128 devices in a mesh: seq: 16 (over y, z), tp: 8 (over x, core).
Axes of the slice: x: 4, y: 4, z: 4, core: 2. Of those that a mesh axis runs over, the one named last changes fastest.
Arguments:
- q_raw: bfloat16 [2048, 8192], P('seq', 'tp'), may hold values from -80 to 80
- out_grad: bfloat16 [2048, 8192], P('seq', 'tp'), may hold values from -384 to 384
- q_gain: float32 [128], replicated, may hold values from 0.1 to 1.9
- image_keys: bfloat16 [16, 6404, 1024], P('seq', None, 'tp'), may hold values from -130 to 130
- image_values: bfloat16 [16, 6404, 1024], P('seq', None, 'tp'), may hold values from -6 to 6
- block_images: int32 [16, 2], replicated, may hold values from -1 to 15, as said below
- image_slot: int32 [16], replicated, may hold values from 0 to 15, as said below
- tile_counts: int32 [16], replicated, may hold values from 1 to 4, as said below
- q_weight: bfloat16 [8192, 8192], P(None, 'tp'), may hold values from -0.0625 to 0.0625
Outputs:
- text_grad: bfloat16 [2048, 8192], P(('seq', 'tp'))
- key_grad: bfloat16 [16, 6404, 1024], P('seq', None, 'tp')
- value_grad: bfloat16 [16, 6404, 1024], P('seq', None, 'tp')
The draws below stay inside these ranges and needn't reach their ends.
Inputs may be any that keep to these rules, and one draw needn't show every extreme that they name: `block_images`: entry 0 over all blocks is a permutation of the image ids. Entry 1 of block 0 is -1, and entry 1 of block b is entry 0 of block b - 1 for b >= 1, so that at most 2 blocks read one image. A permutation: image i is held in row image_slot[i] of image_keys and image_values; that row lies on index image_slot[i] // 1 of seq, the index that holds the text block whose entry 0 is i. Image i uses its first tile_counts[i] * 1601 key rows; the rest are padding that no query reads. Some image has 4 tiles and some has one.
All inputs are finite; a program needn't handle non-finite values.
Results may differ from the reference program's by a relative error of at most 0.02.
The reference program's roundings to bfloat16 on the way (of `normed`, `score_grads`, `probs_low` and `raw_grad`) count: a program that leaves them out, or rounds other values in their place, can miss the bound.
Values may be sent and summed in bfloat16 or wider, within the bound.
A program may use at most 128 MiB of HBM per device.

```python
import math
import jax
import jax.numpy as jnp
from jax import lax

D = 8192
HEADS = 64
KVH = 8
HD = 128
TILE_TOK = 1601
MAX_TILES = 4
TB = 128
LIST = 2
IMG_DEV = 1
TOKENS = 2048
BLOCKS = 16
IMAGES = 16
KEYS = 6404


def shared_order(key):
    return jax.random.permutation(jax.random.fold_in(key, 301), IMAGES).astype(jnp.int32)


def shared_slots(key):
    image_order = shared_order(key)
    groups = jnp.arange(BLOCKS, dtype=jnp.int32).reshape(BLOCKS // IMG_DEV, IMG_DEV)
    mixed = jax.random.permutation(jax.random.fold_in(key, 302), groups, axis=1, independent=True).reshape(BLOCKS)
    return jnp.zeros((IMAGES,), jnp.int32).at[image_order].set(mixed.astype(jnp.int32))


def log_uniform(key, count, lower, upper):
    return jnp.exp(jax.random.uniform(key, (count,), jnp.float32, jnp.log(lower), jnp.log(upper)))


def draw_block_images(key, part):
    image_order = shared_order(key)
    block_ids = jnp.arange(BLOCKS, dtype=jnp.int32)
    previous = jnp.roll(image_order, 1)
    second_entry = jnp.where(block_ids == 0, -1, previous)
    return jnp.stack([image_order, second_entry], axis=1).astype(jnp.int32)


def draw_image_slot(key, part):
    return shared_slots(key)


def draw_tile_counts(key, part):
    key = jax.random.fold_in(key, 3)
    key_a, key_b, key_c = jax.random.split(key, 3)
    counts = jax.random.randint(key_a, (IMAGES,), 1, MAX_TILES + 1)
    largest = jax.random.randint(key_b, (), 0, IMAGES)
    smallest = (largest + 1 + jax.random.randint(key_c, (), 0, IMAGES - 1)) % IMAGES
    counts = counts.at[largest].set(MAX_TILES)
    counts = counts.at[smallest].set(1)
    return counts.astype(jnp.int32)


def draw_q_raw(key, part):
    key = jax.random.fold_in(key, 7)
    key_a, key_b, key_c = jax.random.split(key, 3)
    noise_draw = jnp.clip(jax.random.normal(key_a, (TOKENS, HEADS * HD), jnp.float32), -5.0, 5.0)
    row_scale = log_uniform(key_b, TOKENS, 0.3, 3.0)
    col_scale = log_uniform(key_c, HEADS * HD, 0.3, 3.0)
    return (noise_draw * row_scale[:, None] * col_scale[None, :]).astype(jnp.bfloat16)


def draw_image_keys(key, part):
    key = jax.random.fold_in(key, 11)
    return jnp.clip(jax.random.normal(key, (IMAGES, KEYS, KVH * HD), jnp.float32), -6.0, 6.0).astype(jnp.bfloat16)


def shard_levels(rng, dims, pieces, low, high):
    level, own = 1.0, jax.random.fold_in(rng, 6)
    for position, blocks in pieces:
        draws = jnp.exp(jax.random.uniform(jax.random.fold_in(own, position), (blocks,), jnp.float32, low / len(pieces), high / len(pieces)))
        level = level * jnp.repeat(draws, dims[position] // blocks).reshape([-1 if axis == position else 1 for axis in range(len(dims))])
    return level


def centred(rng, dims, deviation, most, cuts=(), kind=jnp.bfloat16):
    values = jax.random.normal(rng, dims, jnp.float32) * deviation
    if len(cuts) > 0:
        values = shard_levels(rng, dims, cuts, -0.22, 0.18) * values
    return jnp.clip(values, min=-most, max=most).astype(kind)


def setup_inputs(seed: int = 0) -> dict:
    key_of = jax.random.split(jax.random.key(seed), 10)
    return {
        "q_raw": draw_q_raw(jax.random.fold_in(key_of[9], 71), 0),
        "out_grad": centred(key_of[1], (TOKENS, HEADS * HD), 64.0, 384.0, ((0, 16), (1, 8))),
        "q_gain": jnp.clip(1.0 + 0.18 * jax.random.normal(key_of[2], (HD,), jnp.float32), 0.1, 1.9),
        "image_keys": draw_image_keys(jax.random.fold_in(key_of[9], 71), 0),
        "image_values": centred(key_of[4], (IMAGES, KEYS, KVH * HD), 1.0, 6.0, ((0, 16), (2, 8))),
        "block_images": draw_block_images(jax.random.fold_in(key_of[9], 71), 0),
        "image_slot": draw_image_slot(jax.random.fold_in(key_of[9], 71), 0),
        "tile_counts": draw_tile_counts(jax.random.fold_in(key_of[9], 71), 0),
        "q_weight": centred(key_of[8], (D, HEADS * HD), D ** -0.5, 0.0625, ((1, 8),)),
    }


norm_eps = 1e-05

def reference(q_raw, out_grad, q_gain, image_keys, image_values, block_images, image_slot, tile_counts, q_weight):
    group_size = HEADS // KVH
    score_scale = 1.0 / math.sqrt(HD)
    raw_rows = q_raw.astype(jnp.float32).reshape(TOKENS, HEADS, HD)
    inv_rms = lax.rsqrt(lax.optimization_barrier(jnp.mean(raw_rows * raw_rows, axis=-1, keepdims=True)) + norm_eps)
    normed = (raw_rows * inv_rms * q_gain).astype(jnp.bfloat16)
    query_blocks = normed.reshape(BLOCKS, TB, KVH, group_size, HD)
    grad_blocks = out_grad.reshape(BLOCKS, TB, KVH, group_size, HD)
    positions = jnp.arange(KEYS, dtype=jnp.int32)

    def one_block(carry, inputs):
        key_sum, value_sum = carry
        query_block, grad_block, entries = inputs
        is_live = entries >= 0
        safe_ids = jnp.maximum(entries, 0).astype(jnp.int32)
        slot_ids = image_slot[safe_ids].astype(jnp.int32)
        lengths = tile_counts[safe_ids] * TILE_TOK
        allowed = (positions[None, :] < lengths[:, None]) & is_live[:, None]
        flat_allowed = allowed.reshape(LIST * KEYS)
        block_keys = image_keys[slot_ids].reshape(LIST * KEYS, KVH, HD)
        block_values = image_values[slot_ids].reshape(LIST * KEYS, KVH, HD)

        def one_head(kv_head):
            query_f = query_block[:, kv_head].astype(jnp.float32)
            cotan_f = grad_block[:, kv_head].astype(jnp.float32)
            key_f = block_keys[:, kv_head].astype(jnp.float32)
            value_f = block_values[:, kv_head].astype(jnp.float32)
            scores = jnp.einsum('rgh,kh->grk', query_f, key_f) * score_scale
            scores = jnp.where(flat_allowed, scores, -jnp.inf)
            row_top = lax.optimization_barrier(jnp.max(scores, axis=-1, keepdims=True))
            row_lse = row_top + jnp.log(lax.optimization_barrier(jnp.sum(jnp.exp(scores - row_top), axis=-1, keepdims=True)))
            attn_probs = jnp.exp(scores - row_lse)
            slopes = jnp.einsum('rgh,kh->grk', cotan_f, value_f)
            row_delta = lax.optimization_barrier(jnp.sum(attn_probs * slopes, axis=-1, keepdims=True))
            score_grads = lax.optimization_barrier((attn_probs * (slopes - row_delta) * score_scale).astype(jnp.bfloat16)).astype(jnp.float32)
            probs_low = lax.optimization_barrier(attn_probs.astype(jnp.bfloat16)).astype(jnp.float32)
            query_grad = jnp.einsum('grk,kh->rgh', score_grads, key_f)
            key_part = jnp.einsum('grk,rgh->kh', score_grads, query_f)
            value_part = jnp.einsum('grk,rgh->kh', probs_low, cotan_f)
            return (query_grad, key_part, value_part)
        query_grad, key_part, value_part = lax.map(one_head, jnp.arange(KVH, dtype=jnp.int32))
        query_grad = query_grad.transpose(1, 0, 2, 3).reshape(TB, HEADS * HD)
        key_part = key_part.transpose(1, 0, 2).reshape(LIST, KEYS, KVH * HD)
        value_part = value_part.transpose(1, 0, 2).reshape(LIST, KEYS, KVH * HD)
        for entry in range(LIST):
            target = slot_ids[entry]
            key_sum = key_sum.at[target].add(jnp.where(is_live[entry], key_part[entry], 0.0))
            value_sum = value_sum.at[target].add(jnp.where(is_live[entry], value_part[entry], 0.0))
        return ((key_sum, value_sum), query_grad)
    zero_sum = jnp.zeros((IMAGES, KEYS, KVH * HD), jnp.float32)
    (key_sum, value_sum), query_grads = lax.scan(one_block, (zero_sum, zero_sum), (query_blocks, grad_blocks, block_images))
    normed_grad = query_grads.reshape(TOKENS, HEADS, HD)
    scaled = normed_grad * q_gain
    raw_grad = inv_rms * scaled - raw_rows * (inv_rms * inv_rms * inv_rms) * lax.optimization_barrier(jnp.mean(scaled * raw_rows, axis=-1, keepdims=True))
    raw_grad = raw_grad.reshape(TOKENS, HEADS * HD).astype(jnp.bfloat16)
    text_grad = jnp.dot(raw_grad, q_weight.T, preferred_element_type=jnp.float32).astype(jnp.bfloat16)
    return (text_grad, key_sum.astype(jnp.bfloat16), value_sum.astype(jnp.bfloat16))
```

```python
import functools
import math

import jax
import jax.numpy as jnp
from jax import lax
from jax.experimental import pallas as pl
from jax.experimental.pallas import tpu as pltpu
from jax.sharding import PartitionSpec as P

HD = 128
TILE_TOK = 1601
CHUNK = 512
GROUP = 256
norm_eps = 1e-05
score_scale = 1.0 / math.sqrt(HD)
exp2_scale = score_scale * math.log2(math.e)
MESH = pl.DeviceIdType.MESH
bf16, f32 = jnp.bfloat16, jnp.float32


def nn(a, b):
    return jnp.dot(a, b, preferred_element_type=f32)


def nt(a, b):
    return lax.dot_general(a, b, (((1,), (1,)), ((), ())), preferred_element_type=f32)


def attention_kernel(
    limit_ref,
    q_ref,
    g_ref,
    gain_ref,
    key_ref,
    value_ref,
    raw_out,
    key_out,
    value_out,
    keys,
    values,
    keys_t,
    values_t,
    qt,
    gt,
    e_all,
    m_all,
    acc,
    dkt,
    dvt,
    dqt,
    stats_own,
    stats_send,
    stats_in,
    total,
    total_in,
    dq_send,
    dq_in,
    send_sem,
    recv_sem,
):
    seq = lax.axis_index("seq")
    tp = lax.axis_index("tp")
    seq_size = lax.axis_size("seq")
    has_left = seq > 0
    has_next = seq < seq_size - 1
    left = (jnp.maximum(seq - 1, 0), tp)
    right = (jnp.minimum(seq + 1, seq_size - 1), tp)
    heads = q_ref.shape[1] // HD
    cols = q_ref.shape[1]
    key_count = key_ref.shape[1]
    padded = keys.shape[0]
    chunks = padded // CHUNK
    groups = cols // GROUP
    limit = limit_ref[0]

    barrier = pltpu.get_barrier_semaphore()

    for step in (1, seq_size - 1):
        near = (lax.rem(seq + step, seq_size), tp)
        pl.semaphore_signal(barrier, inc=1, device_id=near, device_id_type=MESH)

    def rdma(index, src, dst, device):
        return pltpu.make_async_remote_copy(
            src_ref=src,
            dst_ref=dst,
            send_sem=send_sem.at[index],
            recv_sem=recv_sem.at[index],
            device_id=device,
            device_id_type=MESH,
        )

    q_copy = rdma(0, qt.at[0], qt.at[1], left)
    g_copy = rdma(1, gt.at[0], gt.at[1], left)
    stats_copy = rdma(2, stats_send, stats_in, right)
    total_copy = rdma(3, total.at[0], total_in, left)
    dq_copy = rdma(4, dq_send, dq_in, right)

    gain = gain_ref[...]
    for h in range(heads):
        span = slice(h * HD, (h + 1) * HD)
        raw = q_ref[:, span].astype(f32)
        inv = lax.rsqrt(jnp.mean(raw * raw, axis=-1, keepdims=True) + norm_eps)
        normed = raw * inv * gain
        qt[0, :, span] = normed.T.astype(bf16)
        gt[0, :, span] = g_ref[:, span].T

    pl.semaphore_wait(barrier, 2)

    @pl.when(has_left)
    def _():
        q_copy.start()
        g_copy.start()

    first_key = key_ref[0, 0:1, :]

    def fill(start, rows, key_rows, value_rows):
        held = key_rows.shape[0]
        at = start + lax.broadcasted_iota(jnp.int32, (rows, HD), 0)
        if held < rows:
            pad = jnp.zeros((rows - held, HD), bf16)
            key_rows = jnp.concatenate([key_rows, pad], axis=0)
            value_rows = jnp.concatenate([value_rows, pad], axis=0)
        live = at < limit
        key_f = key_rows.astype(f32)
        value_low = jnp.where(live, value_rows.astype(f32), 0.0).astype(bf16)
        keys[pl.ds(start, rows), :] = jnp.where(live, key_f, first_key.astype(f32)).astype(bf16)
        values[pl.ds(start, rows), :] = value_low
        keys_t[:, pl.ds(start, rows)] = jnp.where(live, key_f, 0.0).astype(bf16).T
        values_t[0:HD, pl.ds(start, rows)] = value_low.T
        live_t = start + lax.broadcasted_iota(jnp.int32, (16, rows), 1) < limit
        values_t[HD : HD + 16, pl.ds(start, rows)] = jnp.where(live_t, 1.0, 0.0).astype(bf16)

    def fill_step(i, carry):
        start = pl.multiple_of(i * CHUNK, CHUNK)
        fill(start, CHUNK, key_ref[0, pl.ds(start, CHUNK), :], value_ref[0, pl.ds(start, CHUNK), :])
        return carry

    whole = key_count // CHUNK
    lax.fori_loop(0, whole, fill_step, 0)
    if whole < chunks:
        tail = whole * CHUNK
        fill(tail, CHUNK, key_ref[0, tail:key_count, :], value_ref[0, tail:key_count, :])

    def totals_pass(b, stats):
        acc[...] = jnp.zeros_like(acc)
        stats[0:1, :] = jnp.full((1, cols), -1e30, f32)

        def step(i, carry):
            start = pl.multiple_of(i * CHUNK, CHUNK)
            key_chunk = keys[pl.ds(start, CHUNK), :]
            value_chunk = values_t[:, pl.ds(start, CHUNK)]

            def product(j):
                return nn(key_chunk, qt[b, :, j * GROUP : (j + 1) * GROUP])

            scores = product(0)
            for j in range(groups):
                later = product(j + 1) if j + 1 < groups else None
                span = slice(j * GROUP, (j + 1) * GROUP)
                before = stats[0:1, span]
                top = jnp.maximum(before, jnp.max(scores, axis=0, keepdims=True) * exp2_scale)
                stats[0:1, span] = top
                m_all[b, i, 0:1, span] = top
                low = jnp.exp2(scores * exp2_scale - top).astype(bf16)
                e_all[b, pl.ds(start, CHUNK), span] = low
                acc[:, span] = acc[:, span] * jnp.exp2(before - top) + nn(value_chunk, low)
                scores = later
            return carry

        lax.fori_loop(0, chunks, step, 0)
        stats[1:2, :] = acc[HD : HD + 1, :]

    def finish_totals(b, stats):
        stats[2:3, :] = jnp.sum(acc[0:HD, :] * gt[b].astype(f32), axis=0, keepdims=True)

    totals_pass(0, stats_own)
    finish_totals(0, stats_own)

    @pl.when(has_next)
    def _():
        q_copy.wait_recv()
        totals_pass(1, stats_send)
        g_copy.wait_recv()
        finish_totals(1, stats_send)
        stats_copy.start()

    @pl.when(has_left)
    def _():
        stats_copy.wait_recv()
        m1, l1, d1 = stats_own[0:1, :], stats_own[1:2, :], stats_own[2:3, :]
        m2, l2, d2 = stats_in[0:1, :], stats_in[1:2, :], stats_in[2:3, :]
        top = jnp.maximum(m1, m2)
        w1, w2 = jnp.exp2(m1 - top), jnp.exp2(m2 - top)
        norm = l1 * w1 + l2 * w2
        total[0, 0:1, :] = top + jnp.log2(norm)
        total[0, 1:2, :] = (d1 * w1 + d2 * w2) / norm
        total_copy.start()

    @pl.when(jnp.logical_not(has_left))
    def _():
        norm = stats_own[1:2, :]
        total[0, 0:1, :] = stats_own[0:1, :] + jnp.log2(norm)
        total[0, 1:2, :] = stats_own[2:3, :] / norm

    def grads_pass(b, totals, write):
        dqt[...] = jnp.zeros_like(dqt)

        def step(i, carry):
            start = pl.multiple_of(i * CHUNK, CHUNK)
            value_chunk = values[pl.ds(start, CHUNK), :]
            key_chunk = keys_t[:, pl.ds(start, CHUNK)]

            def product(j):
                return nn(value_chunk, gt[b, :, j * GROUP : (j + 1) * GROUP])

            slopes = product(0)
            key_part, value_part = None, None
            for j in range(groups):
                later = product(j + 1) if j + 1 < groups else None
                span = slice(j * GROUP, (j + 1) * GROUP)
                weight = jnp.exp2(m_all[b, i, 0:1, span] - totals[0:1, span])
                probs = e_all[b, pl.ds(start, CHUNK), span].astype(f32) * weight
                probs_low = probs.astype(bf16)
                score_grad = (probs * (slopes - totals[1:2, span])).astype(bf16)
                v_part = nt(gt[b, :, span], probs_low)
                k_part = nt(qt[b, :, span], score_grad)
                dqt[:, span] += nn(key_chunk, score_grad)
                key_part = k_part if j == 0 else key_part + k_part
                value_part = v_part if j == 0 else value_part + v_part
                slopes = later
            write(start, key_part, value_part)
            return carry

        lax.fori_loop(0, chunks, step, 0)

    def hold(start, key_part, value_part):
        dkt[:, pl.ds(start, CHUNK)] = key_part
        dvt[:, pl.ds(start, CHUNK)] = value_part

    def emit(start, key_part, value_part):
        hold(start, key_part + dkt[:, pl.ds(start, CHUNK)], value_part + dvt[:, pl.ds(start, CHUNK)])

    @pl.when(has_next)
    def _():
        total_copy.wait_recv()
        grads_pass(1, total_in, hold)
        dq_send[...] = dqt[...].astype(bf16)
        dq_copy.start()

    @pl.when(jnp.logical_not(has_next))
    def _():
        dkt[...] = jnp.zeros_like(dkt)
        dvt[...] = jnp.zeros_like(dvt)

    grads_pass(0, total.at[0], emit)

    def output(start, rows):
        live = start + lax.broadcasted_iota(jnp.int32, (rows, HD), 0) < limit
        span = pl.ds(start, CHUNK)
        key_rows = (dkt[:, span] * score_scale).T[0:rows]
        value_rows = dvt[:, span].T[0:rows]
        key_out[0, pl.ds(start, rows), :] = jnp.where(live, key_rows, 0.0).astype(bf16)
        value_out[0, pl.ds(start, rows), :] = jnp.where(live, value_rows, 0.0).astype(bf16)

    def output_step(i, carry):
        output(pl.multiple_of(i * CHUNK, CHUNK), CHUNK)
        return carry

    lax.fori_loop(0, whole, output_step, 0)
    if whole < chunks:
        output(whole * CHUNK, key_count - whole * CHUNK)

    @pl.when(has_left)
    def _():
        dq_copy.wait_recv()
        dqt[...] += dq_in[...].astype(f32)

    for h in range(heads):
        span = slice(h * HD, (h + 1) * HD)
        raw = q_ref[:, span].astype(f32)
        inv = lax.rsqrt(jnp.mean(raw * raw, axis=-1, keepdims=True) + norm_eps)
        scaled = dqt[:, span].T * score_scale * gain
        spread = jnp.mean(scaled * raw, axis=-1, keepdims=True)
        raw_out[:, span] = (inv * scaled - raw * (inv * inv * inv) * spread).astype(bf16)

    @pl.when(has_left)
    def _():
        q_copy.wait_send()
        g_copy.wait_send()
        total_copy.wait_send()

    @pl.when(has_next)
    def _():
        stats_copy.wait_send()
        dq_copy.wait_send()


def on_device(
    q_raw,
    out_grad,
    q_gain,
    image_keys,
    image_values,
    block_images,
    image_slot,
    tile_counts,
    q_weight,
):
    rows, cols = q_raw.shape
    key_count = image_keys.shape[1]
    padded = -(-key_count // CHUNK) * CHUNK
    chunks = padded // CHUNK
    seq = lax.axis_index("seq")
    limit = jnp.sum(jnp.where(image_slot == seq, tile_counts, 0)).reshape(1) * TILE_TOK
    vmem = pl.BlockSpec(memory_space=pltpu.VMEM)
    V = pltpu.VMEM
    raw_grad, key_grad, value_grad = pl.pallas_call(
        attention_kernel,
        out_shape=(
            jax.ShapeDtypeStruct((rows, cols), bf16),
            jax.ShapeDtypeStruct(image_keys.shape, bf16),
            jax.ShapeDtypeStruct(image_values.shape, bf16),
        ),
        in_specs=[pl.BlockSpec(memory_space=pltpu.SMEM)] + [vmem] * 5,
        out_specs=(vmem, vmem, vmem),
        scratch_shapes=[
            V((padded, HD), bf16),
            V((padded, HD), bf16),
            V((HD, padded), bf16),
            V((HD + 16, padded), bf16),
            V((2, HD, cols), bf16),
            V((2, HD, cols), bf16),
            V((2, padded, cols), bf16),
            V((2, chunks, 8, cols), f32),
            V((HD + 16, cols), f32),
            V((HD, padded), f32),
            V((HD, padded), f32),
            V((HD, cols), f32),
            V((8, cols), f32),
            V((8, cols), f32),
            V((8, cols), f32),
            V((1, 8, cols), f32),
            V((8, cols), f32),
            V((HD, cols), bf16),
            V((HD, cols), bf16),
            pltpu.SemaphoreType.DMA((5,)),
            pltpu.SemaphoreType.DMA((5,)),
        ],
        compiler_params=pltpu.CompilerParams(
            collective_id=0, has_side_effects=True, vmem_limit_bytes=60 << 20
        ),
        name="attention",
    )(limit, q_raw, out_grad, q_gain.reshape(1, HD), image_keys, image_values)
    text_grad = lax.psum_scatter(
        lax.dot_general(
            raw_grad, q_weight, (((1,), (1,)), ((), ())), preferred_element_type=jnp.float32
        ).astype(jnp.bfloat16),
        "tp",
        scatter_dimension=0,
        tiled=True,
    )
    return (text_grad, key_grad, value_grad)


def solution(mesh):
    return jax.shard_map(
        on_device,
        mesh=mesh,
        in_specs=(
            P("seq", "tp"),
            P("seq", "tp"),
            P(),
            P("seq", None, "tp"),
            P("seq", None, "tp"),
            P(),
            P(),
            P(),
            P(None, "tp"),
        ),
        out_specs=(P(("seq", "tp"), None), P("seq", None, "tp"), P("seq", None, "tp")),
        check_vma=False,
    )
```

```python
import functools
import math

import jax
import jax.numpy as jnp
from jax import lax
from jax.experimental import pallas as pl
from jax.experimental.pallas import tpu as pltpu
from jax.sharding import PartitionSpec as P

HD = 128
TILE_TOK = 1601
CHUNK = 512
GROUP = 256
PARTS = 8
norm_eps = 1e-05
score_scale = 1.0 / math.sqrt(HD)
exp2_scale = score_scale * math.log2(math.e)
MESH = pl.DeviceIdType.MESH
bf16, f32 = jnp.bfloat16, jnp.float32


def nn(a, b):
    return jnp.dot(a, b, preferred_element_type=f32)


def nt(a, b):
    return lax.dot_general(a, b, (((1,), (1,)), ((), ())), preferred_element_type=f32)


def attention_kernel(
    limit_ref,
    q_ref,
    g_ref,
    gain_ref,
    key_ref,
    value_ref,
    weight_ref,
    text_out,
    key_out,
    value_out,
    keys,
    values,
    keys_t,
    values_t,
    qt,
    gt,
    e_all,
    m_all,
    acc,
    dkt,
    dvt,
    dqt,
    stats_own,
    stats_send,
    stats_in,
    total,
    total_in,
    dq_send,
    dq_in,
    raw_low,
    weight_tail,
    kept,
    pair_send,
    pair_in,
    far_send,
    far_in,
    near_send,
    near_in,
    weight_sem,
    send_sem,
    recv_sem,
    part_send_sem,
    part_recv_sem,
):
    seq = lax.axis_index("seq")
    tp = lax.axis_index("tp")
    seq_size = lax.axis_size("seq")
    has_left = seq > 0
    has_next = seq < seq_size - 1
    left = (jnp.maximum(seq - 1, 0), tp)
    right = (jnp.minimum(seq + 1, seq_size - 1), tp)
    heads = q_ref.shape[1] // HD
    cols = q_ref.shape[1]
    key_count = key_ref.shape[1]
    padded = keys.shape[0]
    chunks = padded // CHUNK
    groups = cols // GROUP
    limit = limit_ref[0]

    barrier = pltpu.get_barrier_semaphore()

    chips = lax.axis_size("tp") // 2
    chip, core = lax.div(tp, 2), lax.rem(tp, 2)
    pair = (seq, tp + 1 - 2 * core)
    up_chip, down_chip = lax.rem(chip + 1, chips), lax.rem(chip + chips - 1, chips)
    far_chip = lax.rem(chip + 2, chips)
    up, down = (seq, up_chip * 2 + core), (seq, down_chip * 2 + core)
    ahead, behind = lax.rem(seq + 1, seq_size), lax.rem(seq + seq_size - 1, seq_size)
    for near in ((ahead, tp), (behind, tp), pair, up, down):
        pl.semaphore_signal(barrier, inc=1, device_id=near, device_id_type=MESH)

    def rdma(index, src, dst, device):
        return pltpu.make_async_remote_copy(
            src_ref=src,
            dst_ref=dst,
            send_sem=send_sem.at[index],
            recv_sem=recv_sem.at[index],
            device_id=device,
            device_id_type=MESH,
        )

    q_copy = rdma(0, qt.at[0], qt.at[1], left)
    g_copy = rdma(1, gt.at[0], gt.at[1], left)
    stats_copy = rdma(2, stats_send, stats_in, right)
    total_copy = rdma(3, total.at[0], total_in, left)
    dq_copy = rdma(4, dq_send, dq_in, right)

    width = weight_ref.shape[0] // PARTS
    early = (padded // width) * width
    weight_copies = (
        pltpu.make_async_copy(
            weight_ref.at[0:early], e_all.at[1, 0:early], weight_sem.at[0]
        ),
        pltpu.make_async_copy(weight_ref.at[early:], weight_tail, weight_sem.at[1]),
    )
    weight_copies[1].start()

    gain = gain_ref[...]
    for h in range(heads):
        span = slice(h * HD, (h + 1) * HD)
        raw = q_ref[:, span].astype(f32)
        inv = lax.rsqrt(jnp.mean(raw * raw, axis=-1, keepdims=True) + norm_eps)
        normed = raw * inv * gain
        qt[0, :, span] = normed.T.astype(bf16)
        gt[0, :, span] = g_ref[:, span].T

    pl.semaphore_wait(barrier, 5)

    @pl.when(has_left)
    def _():
        q_copy.start()
        g_copy.start()

    first_key = key_ref[0, 0:1, :]

    def fill(start, rows, key_rows, value_rows):
        held = key_rows.shape[0]
        at = start + lax.broadcasted_iota(jnp.int32, (rows, HD), 0)
        if held < rows:
            pad = jnp.zeros((rows - held, HD), bf16)
            key_rows = jnp.concatenate([key_rows, pad], axis=0)
            value_rows = jnp.concatenate([value_rows, pad], axis=0)
        live = at < limit
        key_f = key_rows.astype(f32)
        value_low = jnp.where(live, value_rows.astype(f32), 0.0).astype(bf16)
        keys[pl.ds(start, rows), :] = jnp.where(live, key_f, first_key.astype(f32)).astype(bf16)
        values[pl.ds(start, rows), :] = value_low
        keys_t[:, pl.ds(start, rows)] = jnp.where(live, key_f, 0.0).astype(bf16).T
        values_t[0:HD, pl.ds(start, rows)] = value_low.T
        live_t = start + lax.broadcasted_iota(jnp.int32, (16, rows), 1) < limit
        values_t[HD : HD + 16, pl.ds(start, rows)] = jnp.where(live_t, 1.0, 0.0).astype(bf16)

    def fill_step(i, carry):
        start = pl.multiple_of(i * CHUNK, CHUNK)
        fill(start, CHUNK, key_ref[0, pl.ds(start, CHUNK), :], value_ref[0, pl.ds(start, CHUNK), :])
        return carry

    whole = key_count // CHUNK
    lax.fori_loop(0, whole, fill_step, 0)
    if whole < chunks:
        tail = whole * CHUNK
        fill(tail, CHUNK, key_ref[0, tail:key_count, :], value_ref[0, tail:key_count, :])

    def totals_pass(b, stats):
        acc[...] = jnp.zeros_like(acc)
        stats[0:1, :] = jnp.full((1, cols), -1e30, f32)

        def step(i, carry):
            start = pl.multiple_of(i * CHUNK, CHUNK)
            key_chunk = keys[pl.ds(start, CHUNK), :]
            value_chunk = values_t[:, pl.ds(start, CHUNK)]

            def product(j):
                return nn(key_chunk, qt[b, :, j * GROUP : (j + 1) * GROUP])

            scores = product(0)
            for j in range(groups):
                later = product(j + 1) if j + 1 < groups else None
                span = slice(j * GROUP, (j + 1) * GROUP)
                before = stats[0:1, span]
                top = jnp.maximum(before, jnp.max(scores, axis=0, keepdims=True) * exp2_scale)
                stats[0:1, span] = top
                m_all[b, i, 0:1, span] = top
                low = jnp.exp2(scores * exp2_scale - top).astype(bf16)
                e_all[b, pl.ds(start, CHUNK), span] = low
                acc[:, span] = acc[:, span] * jnp.exp2(before - top) + nn(value_chunk, low)
                scores = later
            return carry

        lax.fori_loop(0, chunks, step, 0)
        stats[1:2, :] = acc[HD : HD + 1, :]

    def finish_totals(b, stats):
        stats[2:3, :] = jnp.sum(acc[0:HD, :] * gt[b].astype(f32), axis=0, keepdims=True)

    totals_pass(0, stats_own)
    finish_totals(0, stats_own)

    @pl.when(has_next)
    def _():
        q_copy.wait_recv()
        totals_pass(1, stats_send)
        g_copy.wait_recv()
        finish_totals(1, stats_send)
        stats_copy.start()

    @pl.when(has_left)
    def _():
        stats_copy.wait_recv()
        m1, l1, d1 = stats_own[0:1, :], stats_own[1:2, :], stats_own[2:3, :]
        m2, l2, d2 = stats_in[0:1, :], stats_in[1:2, :], stats_in[2:3, :]
        top = jnp.maximum(m1, m2)
        w1, w2 = jnp.exp2(m1 - top), jnp.exp2(m2 - top)
        norm = l1 * w1 + l2 * w2
        total[0, 0:1, :] = top + jnp.log2(norm)
        total[0, 1:2, :] = (d1 * w1 + d2 * w2) / norm
        total_copy.start()

    @pl.when(jnp.logical_not(has_left))
    def _():
        norm = stats_own[1:2, :]
        total[0, 0:1, :] = stats_own[0:1, :] + jnp.log2(norm)
        total[0, 1:2, :] = stats_own[2:3, :] / norm

    def grads_pass(b, totals, write):
        dqt[...] = jnp.zeros_like(dqt)

        def step(i, carry):
            start = pl.multiple_of(i * CHUNK, CHUNK)
            value_chunk = values[pl.ds(start, CHUNK), :]
            key_chunk = keys_t[:, pl.ds(start, CHUNK)]

            def product(j):
                return nn(value_chunk, gt[b, :, j * GROUP : (j + 1) * GROUP])

            slopes = product(0)
            key_part, value_part = None, None
            for j in range(groups):
                later = product(j + 1) if j + 1 < groups else None
                span = slice(j * GROUP, (j + 1) * GROUP)
                weight = jnp.exp2(m_all[b, i, 0:1, span] - totals[0:1, span])
                probs = e_all[b, pl.ds(start, CHUNK), span].astype(f32) * weight
                probs_low = probs.astype(bf16)
                score_grad = (probs * (slopes - totals[1:2, span])).astype(bf16)
                v_part = nt(gt[b, :, span], probs_low)
                k_part = nt(qt[b, :, span], score_grad)
                dqt[:, span] += nn(key_chunk, score_grad)
                key_part = k_part if j == 0 else key_part + k_part
                value_part = v_part if j == 0 else value_part + v_part
                slopes = later
            write(start, key_part, value_part)
            return carry

        lax.fori_loop(0, chunks, step, 0)

    def hold(start, key_part, value_part):
        dkt[:, pl.ds(start, CHUNK)] = key_part
        dvt[:, pl.ds(start, CHUNK)] = value_part

    def emit(start, key_part, value_part):
        hold(start, key_part + dkt[:, pl.ds(start, CHUNK)], value_part + dvt[:, pl.ds(start, CHUNK)])

    @pl.when(has_next)
    def _():
        total_copy.wait_recv()
        grads_pass(1, total_in, hold)
        dq_send[...] = dqt[...].astype(bf16)
        dq_copy.start()

    @pl.when(jnp.logical_not(has_next))
    def _():
        dkt[...] = jnp.zeros_like(dkt)
        dvt[...] = jnp.zeros_like(dvt)

    weight_copies[0].start()
    grads_pass(0, total.at[0], emit)

    def output(start, rows):
        live = start + lax.broadcasted_iota(jnp.int32, (rows, HD), 0) < limit
        span = pl.ds(start, CHUNK)
        key_rows = (dkt[:, span] * score_scale).T[0:rows]
        value_rows = dvt[:, span].T[0:rows]
        key_out[0, pl.ds(start, rows), :] = jnp.where(live, key_rows, 0.0).astype(bf16)
        value_out[0, pl.ds(start, rows), :] = jnp.where(live, value_rows, 0.0).astype(bf16)

    def output_step(i, carry):
        output(pl.multiple_of(i * CHUNK, CHUNK), CHUNK)
        return carry

    lax.fori_loop(0, whole, output_step, 0)
    if whole < chunks:
        output(whole * CHUNK, key_count - whole * CHUNK)

    @pl.when(has_left)
    def _():
        dq_copy.wait_recv()
        dqt[...] += dq_in[...].astype(f32)

    for h in range(heads):
        span = slice(h * HD, (h + 1) * HD)
        raw = q_ref[:, span].astype(f32)
        inv = lax.rsqrt(jnp.mean(raw * raw, axis=-1, keepdims=True) + norm_eps)
        scaled = dqt[:, span].T * score_scale * gain
        spread = jnp.mean(scaled * raw, axis=-1, keepdims=True)
        raw_low[:, span] = (inv * scaled - raw * (inv * inv * inv) * spread).astype(bf16)

    half = width // 2

    def part_copy(kind, n, src, dst, device):
        return pltpu.make_async_remote_copy(
            src_ref=src,
            dst_ref=dst,
            send_sem=part_send_sem.at[kind, n],
            recv_sem=part_recv_sem.at[kind, n],
            device_id=device,
            device_id_type=MESH,
        )

    def pair_copy(n):
        return part_copy(0, n, pair_send.at[n], pair_in.at[n], pair)

    def far_copies(n):
        return (
            part_copy(1, n, far_send.at[0, n], far_in.at[0, n], up),
            part_copy(2, n, far_send.at[1, n], far_in.at[1, n], down),
        )

    def near_copies(n):
        return (
            part_copy(3, n, near_send.at[0, n], near_in.at[0, n], up),
            part_copy(4, n, near_send.at[1, n], near_in.at[1, n], down),
        )

    def multiply(n):
        if (n + 1) * width <= early:
            rows = e_all[1, n * width : (n + 1) * width, :]
        else:
            rows = weight_tail[n * width - early : (n + 1) * width - early, :]
        product = nt(raw_low[...], rows).reshape(chips, 2, 16, width)
        first, second = product[:, 0], product[:, 1]
        kept[n] = jnp.where(core == 0, first, second)
        pair_send[n] = jnp.where(core == 0, second, first).astype(bf16)
        pair_copy(n).start()

    def send_far(n):
        pair_copy(n).wait_recv()
        kept[n] = kept[n] + pair_in[n].astype(f32)
        far = kept[n, far_chip].astype(bf16)
        far_send[0, n] = far[:, 0:half]
        far_send[1, n] = far[:, half:width]
        for copy in far_copies(n):
            copy.start()

    def send_near(n):
        for copy in far_copies(n):
            copy.wait_recv()
        one, other = kept[n, up_chip], kept[n, down_chip]
        near_send[0, n, :, 0:half] = (one[:, 0:half] + far_in[0, n].astype(f32)).astype(bf16)
        near_send[0, n, :, half:width] = one[:, half:width].astype(bf16)
        near_send[1, n, :, 0:half] = other[:, 0:half].astype(bf16)
        near_send[1, n, :, half:width] = (other[:, half:width] + far_in[1, n].astype(f32)).astype(bf16)
        for copy in near_copies(n):
            copy.start()

    def finish(n):
        for copy in near_copies(n):
            copy.wait_recv()
        whole_sum = kept[n, chip] + near_in[0, n].astype(f32) + near_in[1, n].astype(f32)
        text_out[:, n * width : (n + 1) * width] = whole_sum.astype(bf16)

    for copy in weight_copies:
        copy.wait()
    for t in range(PARTS + 10):
        for lag, stage in ((0, multiply), (3, send_far), (6, send_near), (10, finish)):
            if 0 <= t - lag < PARTS:
                stage(t - lag)
    for n in range(PARTS):
        for copy in (pair_copy(n), *far_copies(n), *near_copies(n)):
            copy.wait_send()

    @pl.when(has_left)
    def _():
        q_copy.wait_send()
        g_copy.wait_send()
        total_copy.wait_send()

    @pl.when(has_next)
    def _():
        stats_copy.wait_send()
        dq_copy.wait_send()


def on_device(
    q_raw,
    out_grad,
    q_gain,
    image_keys,
    image_values,
    block_images,
    image_slot,
    tile_counts,
    q_weight,
):
    rows, cols = q_raw.shape
    key_count = image_keys.shape[1]
    padded = -(-key_count // CHUNK) * CHUNK
    chunks = padded // CHUNK
    seq = lax.axis_index("seq")
    limit = jnp.sum(jnp.where(image_slot == seq, tile_counts, 0)).reshape(1) * TILE_TOK
    vmem = pl.BlockSpec(memory_space=pltpu.VMEM)
    V = pltpu.VMEM
    width = q_weight.shape[0] // PARTS
    weight_rest = q_weight.shape[0] - padded // width * width
    chips = lax.axis_size("tp") // 2
    return pl.pallas_call(
        attention_kernel,
        out_shape=(
            jax.ShapeDtypeStruct((rows // (2 * chips), q_weight.shape[0]), bf16),
            jax.ShapeDtypeStruct(image_keys.shape, bf16),
            jax.ShapeDtypeStruct(image_values.shape, bf16),
        ),
        in_specs=[pl.BlockSpec(memory_space=pltpu.SMEM)] + [vmem] * 5 + [pl.BlockSpec(memory_space=pl.ANY)],
        out_specs=(vmem, vmem, vmem),
        scratch_shapes=[
            V((padded, HD), bf16),
            V((padded, HD), bf16),
            V((HD, padded), bf16),
            V((HD + 16, padded), bf16),
            V((2, HD, cols), bf16),
            V((2, HD, cols), bf16),
            V((2, padded, cols), bf16),
            V((2, chunks, 1, cols), f32),
            V((HD + 16, cols), f32),
            V((HD, padded), f32),
            V((HD, padded), f32),
            V((HD, cols), f32),
            V((8, cols), f32),
            V((8, cols), f32),
            V((8, cols), f32),
            V((1, 8, cols), f32),
            V((8, cols), f32),
            V((HD, cols), bf16),
            V((HD, cols), bf16),
            V((rows, cols), bf16),
            V((weight_rest, cols), bf16),
            V((PARTS, chips, 16, width), f32),
            V((PARTS, chips, 16, width), bf16),
            V((PARTS, chips, 16, width), bf16),
            V((2, PARTS, 16, width // 2), bf16),
            V((2, PARTS, 16, width // 2), bf16),
            V((2, PARTS, 16, width), bf16),
            V((2, PARTS, 16, width), bf16),
            pltpu.SemaphoreType.DMA((2,)),
            pltpu.SemaphoreType.DMA((5,)),
            pltpu.SemaphoreType.DMA((5,)),
            pltpu.SemaphoreType.DMA((5, PARTS)),
            pltpu.SemaphoreType.DMA((5, PARTS)),
        ],
        compiler_params=pltpu.CompilerParams(
            collective_id=0, has_side_effects=True, vmem_limit_bytes=63 << 20
        ),
        name="attention",
    )(limit, q_raw, out_grad, q_gain.reshape(1, HD), image_keys, image_values, q_weight)


def solution(mesh):
    return jax.shard_map(
        on_device,
        mesh=mesh,
        in_specs=(
            P("seq", "tp"),
            P("seq", "tp"),
            P(),
            P("seq", None, "tp"),
            P("seq", None, "tp"),
            P(),
            P(),
            P(),
            P(None, "tp"),
        ),
        out_specs=(P(("seq", "tp"), None), P("seq", None, "tp"), P("seq", None, "tp")),
        check_vma=False,
    )
```

```python
import functools
import math

import jax
import jax.numpy as jnp
from jax import lax
from jax.experimental import pallas as pl
from jax.experimental.pallas import tpu as pltpu
from jax.sharding import PartitionSpec as P

HD = 128
TILE_TOK = 1601
CHUNK = 512
GROUP = 256
PARTS = 8
norm_eps = 1e-05
score_scale = 1.0 / math.sqrt(HD)
exp2_scale = score_scale * math.log2(math.e)
MESH = pl.DeviceIdType.MESH
bf16, f32 = jnp.bfloat16, jnp.float32


def nn(a, b):
    return jnp.dot(a, b, preferred_element_type=f32)


def nt(a, b):
    return lax.dot_general(a, b, (((1,), (1,)), ((), ())), preferred_element_type=f32)


def attention_kernel(
    slot_ref,
    tiles_ref,
    q_ref,
    g_ref,
    gain_ref,
    key_ref,
    value_ref,
    weight_ref,
    text_out,
    key_out,
    value_out,
    key_rows_ref,
    value_rows_ref,
    keys,
    values,
    keys_t,
    values_t,
    qt,
    gt,
    e_all,
    m_all,
    held,
    probs_t,
    grads_t,
    acc,
    dkt,
    dvt,
    dqt,
    stats_own,
    stats_send,
    stats_in,
    total,
    total_in,
    dq_send,
    dq_in,
    raw_low,
    weight_tail,
    pair_send,
    pair_in,
    far_send,
    far_in,
    near_send,
    near_in,
    local_sem,
    send_sem,
    recv_sem,
    part_send_sem,
    part_recv_sem,
):
    seq = lax.axis_index("seq")
    tp = lax.axis_index("tp")
    seq_size = lax.axis_size("seq")
    has_left = seq > 0
    has_next = seq < seq_size - 1
    left = (jnp.maximum(seq - 1, 0), tp)
    right = (jnp.minimum(seq + 1, seq_size - 1), tp)
    heads = q_ref.shape[1] // HD
    cols = q_ref.shape[1]
    key_count = key_ref.shape[1]
    padded = keys.shape[0]
    chunks = padded // CHUNK
    groups = cols // GROUP
    limit = jnp.int32(0)
    for i in range(slot_ref.shape[0]):
        limit += jnp.where(slot_ref[i] == seq, tiles_ref[i], 0)
    limit = limit * TILE_TOK

    barrier = pltpu.get_barrier_semaphore()

    chips = lax.axis_size("tp") // 2
    chip, core = lax.div(tp, 2), lax.rem(tp, 2)
    pair = (seq, tp + 1 - 2 * core)
    up_chip, down_chip = lax.rem(chip + 1, chips), lax.rem(chip + chips - 1, chips)
    far_chip = lax.rem(chip + 2, chips)
    up, down = (seq, up_chip * 2 + core), (seq, down_chip * 2 + core)
    ahead, behind = lax.rem(seq + 1, seq_size), lax.rem(seq + seq_size - 1, seq_size)
    for near in ((ahead, tp), (behind, tp), pair, up, down):
        pl.semaphore_signal(barrier, inc=1, device_id=near, device_id_type=MESH)

    def rdma(index, src, dst, device):
        return pltpu.make_async_remote_copy(
            src_ref=src,
            dst_ref=dst,
            send_sem=send_sem.at[index],
            recv_sem=recv_sem.at[index],
            device_id=device,
            device_id_type=MESH,
        )

    q_copy = rdma(0, qt.at[0], qt.at[1], left)
    g_copy = rdma(1, gt.at[0], gt.at[1], left)
    stats_copy = rdma(2, stats_send, stats_in, right)
    total_copy = rdma(3, total.at[0], total_in, left)
    dq_copy = rdma(4, dq_send, dq_in, right)

    width = weight_ref.shape[0] // PARTS
    early = (padded // width) * width
    weight_copies = (
        pltpu.make_async_copy(
            weight_ref.at[0:early], e_all.at[1, 0:early], local_sem.at[0]
        ),
        pltpu.make_async_copy(weight_ref.at[early:], weight_tail, local_sem.at[1]),
    )
    row_copies = (
        pltpu.make_async_copy(key_ref.at[0], key_rows_ref, local_sem.at[2]),
        pltpu.make_async_copy(value_ref.at[0], value_rows_ref, local_sem.at[3]),
    )
    out_copies = (
        pltpu.make_async_copy(key_rows_ref, key_out.at[0], local_sem.at[4]),
        pltpu.make_async_copy(value_rows_ref, value_out.at[0], local_sem.at[5]),
    )
    for copy in row_copies:
        copy.start()
    weight_copies[1].start()

    gain = gain_ref[...]
    for h in range(heads):
        span = slice(h * HD, (h + 1) * HD)
        raw = q_ref[:, span].astype(f32)
        inv = lax.rsqrt(jnp.mean(raw * raw, axis=-1, keepdims=True) + norm_eps)
        normed = raw * inv * gain
        qt[0, :, span] = normed.T.astype(bf16)

    pl.semaphore_wait(barrier, 5)

    @pl.when(has_left)
    def _():
        q_copy.start()

    for h in range(heads):
        span = slice(h * HD, (h + 1) * HD)
        gt[0, :, span] = g_ref[:, span].T
    for copy in row_copies:
        copy.wait()
    first_key = key_rows_ref[0:1, :]

    def fill(start, rows, key_rows, value_rows):
        held = key_rows.shape[0]
        at = start + lax.broadcasted_iota(jnp.int32, (rows, HD), 0)
        if held < rows:
            pad = jnp.zeros((rows - held, HD), bf16)
            key_rows = jnp.concatenate([key_rows, pad], axis=0)
            value_rows = jnp.concatenate([value_rows, pad], axis=0)
        live = at < limit
        key_f = key_rows.astype(f32)
        value_low = jnp.where(live, value_rows.astype(f32), 0.0).astype(bf16)
        keys[pl.ds(start, rows), :] = jnp.where(live, key_f, first_key.astype(f32)).astype(bf16)
        values[pl.ds(start, rows), :] = value_low
        keys_t[:, pl.ds(start, rows)] = jnp.where(live, key_f, 0.0).astype(bf16).T
        values_t[0:HD, pl.ds(start, rows)] = value_low.T
        live_t = start + lax.broadcasted_iota(jnp.int32, (16, rows), 1) < limit
        values_t[HD : HD + 16, pl.ds(start, rows)] = jnp.where(live_t, 1.0, 0.0).astype(bf16)

    def fill_chunk(i):
        start = pl.multiple_of(i * CHUNK, CHUNK)
        span = pl.ds(start, CHUNK)
        fill(start, CHUNK, key_rows_ref[span, :], value_rows_ref[span, :])

    whole = key_count // CHUNK
    if whole < chunks:
        tail = whole * CHUNK
        fill(tail, CHUNK, key_rows_ref[tail:key_count, :], value_rows_ref[tail:key_count, :])
    fill_chunk(0)
    fill_chunk(1)

    def columns(j):
        return slice(j * GROUP, (j + 1) * GROUP)

    def chunk_start(i):
        return pl.multiple_of(i * CHUNK, CHUNK)

    def totals_pass(b, stats):
        def scores_of(start, j):
            return nn(keys[pl.ds(start, CHUNK), :], qt[b, :, columns(j)])

        for j in range(groups):
            first = scores_of(0, j)
            held[:, columns(j)] = first
            stats[0:1, columns(j)] = jnp.max(first, axis=0, keepdims=True) * exp2_scale
        stats[1:2, :] = stats[0:1, :]
        acc[...] = jnp.zeros_like(acc)

        def step(i, carry, last=False):
            start = chunk_start(i)
            value_chunk = values_t[:, pl.ds(start, CHUNK)]
            if b == 0 and not last:
                fill_chunk(jnp.minimum(i + 2, whole - 1))
            for j in range(groups):
                span = columns(j)
                top = stats[0:1, span]
                before = stats[1:2, span]
                low = jnp.exp2(held[:, span] * exp2_scale - top).astype(bf16)
                m_all[b, i, 0:1, span] = top
                e_all[b, pl.ds(start, CHUNK), span] = low
                if not last:
                    later = scores_of(chunk_start(i + 1), j)
                    held[:, span] = later
                    stats[0:1, span] = jnp.maximum(
                        top, jnp.max(later, axis=0, keepdims=True) * exp2_scale
                    )
                    stats[1:2, span] = top
                acc[:, span] = acc[:, span] * jnp.exp2(before - top) + nn(value_chunk, low)
            return carry

        lax.fori_loop(0, chunks - 1, step, 0)
        step(chunks - 1, 0, True)
        stats[1:2, :] = acc[HD : HD + 1, :]

    def finish_totals(b, stats):
        stats[2:3, :] = jnp.sum(acc[0:HD, :] * gt[b].astype(f32), axis=0, keepdims=True)

    totals_pass(0, stats_own)

    @pl.when(has_left)
    def _():
        g_copy.start()

    finish_totals(0, stats_own)

    @pl.when(has_next)
    def _():
        q_copy.wait_recv()
        totals_pass(1, stats_send)
        g_copy.wait_recv()
        finish_totals(1, stats_send)
        stats_copy.start()

    @pl.when(has_left)
    def _():
        stats_copy.wait_recv()
        m1, l1, d1 = stats_own[0:1, :], stats_own[1:2, :], stats_own[2:3, :]
        m2, l2, d2 = stats_in[0:1, :], stats_in[1:2, :], stats_in[2:3, :]
        top = jnp.maximum(m1, m2)
        w1, w2 = jnp.exp2(m1 - top), jnp.exp2(m2 - top)
        norm = l1 * w1 + l2 * w2
        total[0, 0:1, :] = top + jnp.log2(norm)
        total[0, 1:2, :] = (d1 * w1 + d2 * w2) / norm
        total_copy.start()

    @pl.when(jnp.logical_not(has_left))
    def _():
        norm = stats_own[1:2, :]
        total[0, 0:1, :] = stats_own[0:1, :] + jnp.log2(norm)
        total[0, 1:2, :] = stats_own[2:3, :] / norm

    def grads_pass(b, totals, write):
        def slopes_of(start, j):
            return nn(values[pl.ds(start, CHUNK), :], gt[b, :, columns(j)])

        for j in range(groups):
            held[:, columns(j)] = slopes_of(0, j)
        dqt[...] = jnp.zeros_like(dqt)

        def step(i, carry, last=False):
            start = chunk_start(i)
            key_chunk = keys_t[:, pl.ds(start, CHUNK)]
            key_part, value_part = None, None
            for j in range(groups):
                span = columns(j)
                weight = jnp.exp2(m_all[b, i, 0:1, span] - totals[0:1, span])
                probs = e_all[b, pl.ds(start, CHUNK), span].astype(f32) * weight
                probs_low = probs.astype(bf16)
                score_grad = (probs * (held[:, span] - totals[1:2, span])).astype(bf16)
                if not last:
                    held[:, span] = slopes_of(chunk_start(i + 1), j)
                probs_t[span, :] = probs_low.T
                grads_t[span, :] = score_grad.T
                v_part = nn(gt[b, :, span], probs_t[span, :])
                k_part = nn(qt[b, :, span], grads_t[span, :])
                dqt[:, span] += nn(key_chunk, score_grad)
                key_part = k_part if j == 0 else key_part + k_part
                value_part = v_part if j == 0 else value_part + v_part
            write(start, key_part, value_part)
            return carry

        lax.fori_loop(0, chunks - 1, step, 0)
        step(chunks - 1, 0, True)

    def hold(start, key_part, value_part):
        dkt[:, pl.ds(start, CHUNK)] = key_part
        dvt[:, pl.ds(start, CHUNK)] = value_part

    def emit(start, key_part, value_part):
        hold(start, key_part + dkt[:, pl.ds(start, CHUNK)], value_part + dvt[:, pl.ds(start, CHUNK)])

    @pl.when(has_next)
    def _():
        total_copy.wait_recv()
        grads_pass(1, total_in, hold)
        dq_send[...] = dqt[...].astype(bf16)
        dq_copy.start()

    @pl.when(jnp.logical_not(has_next))
    def _():
        dkt[...] = jnp.zeros_like(dkt)
        dvt[...] = jnp.zeros_like(dvt)

    weight_copies[0].start()
    grads_pass(0, total.at[0], emit)

    def output(i):
        start = i * CHUNK
        rows = min(CHUNK, key_count - start)
        live = start + lax.broadcasted_iota(jnp.int32, (rows, HD), 0) < limit
        span = slice(start, start + CHUNK)
        key_rows = (dkt[:, span] * score_scale).T[0:rows]
        value_rows = dvt[:, span].T[0:rows]
        key_rows_ref[start : start + rows, :] = jnp.where(live, key_rows, 0.0).astype(bf16)
        value_rows_ref[start : start + rows, :] = jnp.where(live, value_rows, 0.0).astype(bf16)
        if i == chunks - 1:
            for copy in out_copies:
                copy.start()

    @pl.when(has_left)
    def _():
        dq_copy.wait_recv()
        dqt[...] += dq_in[...].astype(f32)

    for h in range(heads):
        span = slice(h * HD, (h + 1) * HD)
        raw = q_ref[:, span].astype(f32)
        inv = lax.rsqrt(jnp.mean(raw * raw, axis=-1, keepdims=True) + norm_eps)
        scaled = dqt[:, span].T * score_scale * gain
        spread = jnp.mean(scaled * raw, axis=-1, keepdims=True)
        raw_low[:, span] = (inv * scaled - raw * (inv * inv * inv) * spread).astype(bf16)

    half = width // 2

    def part_copy(kind, n, src, dst, device):
        return pltpu.make_async_remote_copy(
            src_ref=src,
            dst_ref=dst,
            send_sem=part_send_sem.at[kind, n],
            recv_sem=part_recv_sem.at[kind, n],
            device_id=device,
            device_id_type=MESH,
        )

    def pair_copy(n):
        return part_copy(0, n, pair_send.at[n], pair_in.at[n], pair)

    def far_copies(n):
        return (
            part_copy(1, n, far_send.at[0, n], far_in.at[0, n], up),
            part_copy(2, n, far_send.at[1, n], far_in.at[1, n], down),
        )

    def near_copies(n):
        return (
            part_copy(3, n, near_send.at[0, n], near_in.at[0, n], up),
            part_copy(4, n, near_send.at[1, n], near_in.at[1, n], down),
        )

    def kept(n, place):
        return pl.ds(pl.multiple_of((n * chips + place) * 16, 16), 16)

    def multiply(n):
        if (n + 1) * width <= early:
            rows = e_all[1, n * width : (n + 1) * width, :]
        else:
            rows = weight_tail[n * width - early : (n + 1) * width - early, :]
        product = nt(raw_low[...], rows).reshape(chips, 2, 16, width)
        first, second = product[:, 0], product[:, 1]
        held[n * chips * 16 : (n + 1) * chips * 16, :] = jnp.where(
            core == 0, first, second
        ).reshape(chips * 16, width)
        pair_send[n] = jnp.where(core == 0, second, first).astype(bf16)
        pair_copy(n).start()

    def send_far(n):
        pair_copy(n).wait_recv()
        held[n * chips * 16 : (n + 1) * chips * 16, :] += (
            pair_in[n].astype(f32).reshape(chips * 16, width)
        )
        far = held[kept(n, far_chip), :].astype(bf16)
        far_send[0, n] = far[:, 0:half]
        far_send[1, n] = far[:, half:width]
        for copy in far_copies(n):
            copy.start()

    def send_near(n):
        for copy in far_copies(n):
            copy.wait_recv()
        one, other = held[kept(n, up_chip), :], held[kept(n, down_chip), :]
        near_send[0, n, :, 0:half] = (one[:, 0:half] + far_in[0, n].astype(f32)).astype(bf16)
        near_send[0, n, :, half:width] = one[:, half:width].astype(bf16)
        near_send[1, n, :, 0:half] = other[:, 0:half].astype(bf16)
        near_send[1, n, :, half:width] = (other[:, half:width] + far_in[1, n].astype(f32)).astype(bf16)
        for copy in near_copies(n):
            copy.start()

    def finish(n):
        for copy in near_copies(n):
            copy.wait_recv()
        whole_sum = held[kept(n, chip), :] + near_in[0, n].astype(f32) + near_in[1, n].astype(f32)
        text_out[:, n * width : (n + 1) * width] = whole_sum.astype(bf16)

    for copy in weight_copies:
        copy.wait()
    for t in range(PARTS + 10):
        for lag, stage in ((0, multiply), (3, send_far), (6, send_near), (10, finish)):
            if 0 <= t - lag < PARTS:
                stage(t - lag)
        if 3 <= t < chunks + 3:
            output(t - 3)
    for copy in out_copies:
        copy.wait()
    for n in range(PARTS):
        for copy in (pair_copy(n), *far_copies(n), *near_copies(n)):
            copy.wait_send()

    @pl.when(has_left)
    def _():
        q_copy.wait_send()
        g_copy.wait_send()
        total_copy.wait_send()

    @pl.when(has_next)
    def _():
        stats_copy.wait_send()
        dq_copy.wait_send()


def hand_over_kernel(
    text_in, key_in, value_in, text_out, key_out, value_out, text, keys, values, in_sem, out_sem
):
    held = (text, keys, values)
    arrive = [
        pltpu.make_async_copy(src, dst, in_sem.at[n])
        for n, (src, dst) in enumerate(zip((text_in, key_in, value_in), held))
    ]
    leave = [
        pltpu.make_async_copy(src, dst, out_sem.at[n])
        for n, (src, dst) in enumerate(zip(held, (text_out, key_out, value_out)))
    ]
    for copy in arrive:
        copy.start()
    for first, second in zip(arrive, leave):
        first.wait()
        second.start()
    for copy in leave:
        copy.wait()


def on_device(
    q_raw,
    out_grad,
    q_gain,
    image_keys,
    image_values,
    block_images,
    image_slot,
    tile_counts,
    q_weight,
):
    rows, cols = q_raw.shape
    key_count = image_keys.shape[1]
    padded = -(-key_count // CHUNK) * CHUNK
    chunks = padded // CHUNK
    smem = pl.BlockSpec(memory_space=pltpu.SMEM)
    vmem = pl.BlockSpec(memory_space=pltpu.VMEM)
    hbm = pl.BlockSpec(memory_space=pl.ANY)
    V = pltpu.VMEM
    width = q_weight.shape[0] // PARTS
    weight_rest = q_weight.shape[0] - padded // width * width
    chips = lax.axis_size("tp") // 2
    results = pl.pallas_call(
        attention_kernel,
        out_shape=(
            jax.ShapeDtypeStruct((rows // (2 * chips), q_weight.shape[0]), bf16),
            jax.ShapeDtypeStruct(image_keys.shape, bf16),
            jax.ShapeDtypeStruct(image_values.shape, bf16),
        ),
        in_specs=[smem] * 2 + [vmem] * 3 + [hbm] * 3,
        out_specs=(vmem, hbm, hbm),
        scratch_shapes=[
            V((key_count, HD), bf16),
            V((key_count, HD), bf16),
            V((padded, HD), bf16),
            V((padded, HD), bf16),
            V((HD, padded), bf16),
            V((HD + 16, padded), bf16),
            V((2, HD, cols), bf16),
            V((2, HD, cols), bf16),
            V((2, padded, cols), bf16),
            V((2, chunks, 1, cols), f32),
            V((CHUNK, cols), f32),
            V((cols, CHUNK), bf16),
            V((cols, CHUNK), bf16),
            V((HD + 16, cols), f32),
            V((HD, padded), f32),
            V((HD, padded), f32),
            V((HD, cols), f32),
            V((8, cols), f32),
            V((8, cols), f32),
            V((8, cols), f32),
            V((1, 8, cols), f32),
            V((8, cols), f32),
            V((HD, cols), bf16),
            V((HD, cols), bf16),
            V((rows, cols), bf16),
            V((weight_rest, cols), bf16),
            V((PARTS, chips, 16, width), bf16),
            V((PARTS, chips, 16, width), bf16),
            V((2, PARTS, 16, width // 2), bf16),
            V((2, PARTS, 16, width // 2), bf16),
            V((2, PARTS, 16, width), bf16),
            V((2, PARTS, 16, width), bf16),
            pltpu.SemaphoreType.DMA((6,)),
            pltpu.SemaphoreType.DMA((5,)),
            pltpu.SemaphoreType.DMA((5,)),
            pltpu.SemaphoreType.DMA((5, PARTS)),
            pltpu.SemaphoreType.DMA((5, PARTS)),
        ],
        compiler_params=pltpu.CompilerParams(
            collective_id=0, has_side_effects=True, vmem_limit_bytes=63 << 20
        ),
        name="attention",
    )(image_slot, tile_counts, q_raw, out_grad, q_gain.reshape(1, HD), image_keys, image_values, q_weight)
    return pl.pallas_call(
        hand_over_kernel,
        out_shape=tuple(jax.ShapeDtypeStruct(x.shape, x.dtype) for x in results),
        in_specs=[hbm] * 3,
        out_specs=(hbm, hbm, hbm),
        scratch_shapes=[V(x.shape, x.dtype) for x in results]
        + [pltpu.SemaphoreType.DMA((3,))] * 2,
        compiler_params=pltpu.CompilerParams(vmem_limit_bytes=63 << 20),
        name="hand_over",
    )(*results)


def solution(mesh):
    return jax.shard_map(
        on_device,
        mesh=mesh,
        in_specs=(
            P("seq", "tp"),
            P("seq", "tp"),
            P(),
            P("seq", None, "tp"),
            P("seq", None, "tp"),
            P(),
            P(),
            P(),
            P(None, "tp"),
        ),
        out_specs=(P(("seq", "tp"), None), P("seq", None, "tp"), P("seq", None, "tp")),
        check_vma=False,
    )
```

```python
import functools
import math

import jax
import jax.numpy as jnp
from jax import lax
from jax.experimental import pallas as pl
from jax.experimental.pallas import tpu as pltpu
from jax.sharding import PartitionSpec as P

HD = 128
TILE_TOK = 1601
CHUNK = 512
GROUP = 256
PARTS = 8
norm_eps = 1e-05
score_scale = 1.0 / math.sqrt(HD)
exp2_scale = score_scale * math.log2(math.e)
MESH = pl.DeviceIdType.MESH
bf16, f32 = jnp.bfloat16, jnp.float32


def nn(a, b):
    return jnp.dot(a, b, preferred_element_type=f32)


def nt(a, b):
    return lax.dot_general(a, b, (((1,), (1,)), ((), ())), preferred_element_type=f32)


def attention_kernel(
    slot_ref,
    tiles_ref,
    q_ref,
    g_ref,
    gain_ref,
    key_ref,
    value_ref,
    weight_ref,
    text_out,
    key_out,
    value_out,
    key_rows_ref,
    value_rows_ref,
    keys,
    values,
    keys_t,
    values_t,
    qt,
    gt,
    e_all,
    m_all,
    held,
    probs_t,
    grads_t,
    acc,
    dkt,
    dvt,
    dqt,
    stats_own,
    stats_send,
    stats_in,
    total,
    total_in,
    dq_send,
    dq_in,
    raw_low,
    weight_tail,
    pair_send,
    pair_in,
    far_send,
    far_in,
    near_send,
    near_in,
    local_sem,
    send_sem,
    recv_sem,
    part_send_sem,
    part_recv_sem,
):
    seq = lax.axis_index("seq")
    tp = lax.axis_index("tp")
    seq_size = lax.axis_size("seq")
    has_left = seq > 0
    has_next = seq < seq_size - 1
    left = (jnp.maximum(seq - 1, 0), tp)
    right = (jnp.minimum(seq + 1, seq_size - 1), tp)
    heads = q_ref.shape[1] // HD
    cols = q_ref.shape[1]
    key_count = key_ref.shape[1]
    padded = keys.shape[0]
    chunks = padded // CHUNK
    groups = cols // GROUP
    own_totals = chunks * 2 // 3
    own_grads = chunks // 4
    limit = jnp.int32(0)
    for i in range(slot_ref.shape[0]):
        limit += jnp.where(slot_ref[i] == seq, tiles_ref[i], 0)
    limit = limit * TILE_TOK

    barrier = pltpu.get_barrier_semaphore()

    chips = lax.axis_size("tp") // 2
    chip, core = lax.div(tp, 2), lax.rem(tp, 2)
    pair = (seq, tp + 1 - 2 * core)
    up_chip, down_chip = lax.rem(chip + 1, chips), lax.rem(chip + chips - 1, chips)
    far_chip = lax.rem(chip + 2, chips)
    up, down = (seq, up_chip * 2 + core), (seq, down_chip * 2 + core)
    ahead, behind = lax.rem(seq + 1, seq_size), lax.rem(seq + seq_size - 1, seq_size)
    for near in ((ahead, tp), (behind, tp), pair, up, down):
        pl.semaphore_signal(barrier, inc=1, device_id=near, device_id_type=MESH)

    def rdma(index, src, dst, device):
        return pltpu.make_async_remote_copy(
            src_ref=src,
            dst_ref=dst,
            send_sem=send_sem.at[index],
            recv_sem=recv_sem.at[index],
            device_id=device,
            device_id_type=MESH,
        )

    q_copy = rdma(0, qt.at[0], qt.at[1], left)
    g_copy = rdma(1, gt.at[0], gt.at[1], left)
    stats_copy = rdma(2, stats_send, stats_in, right)
    total_copy = rdma(3, total.at[0], total_in, left)
    dq_copy = rdma(4, dq_send, dq_in, right)

    width = weight_ref.shape[0] // PARTS
    early = (padded // width) * width
    weight_copies = (
        pltpu.make_async_copy(
            weight_ref.at[0:early], e_all.at[1, 0:early], local_sem.at[0]
        ),
        pltpu.make_async_copy(weight_ref.at[early:], weight_tail, local_sem.at[1]),
    )
    row_copies = (
        pltpu.make_async_copy(key_ref.at[0], key_rows_ref, local_sem.at[2]),
        pltpu.make_async_copy(value_ref.at[0], value_rows_ref, local_sem.at[3]),
    )
    out_copies = (
        pltpu.make_async_copy(key_rows_ref, key_out.at[0], local_sem.at[4]),
        pltpu.make_async_copy(value_rows_ref, value_out.at[0], local_sem.at[5]),
    )
    for copy in row_copies:
        copy.start()
    weight_copies[1].start()

    gain = gain_ref[...]
    for h in range(heads):
        span = slice(h * HD, (h + 1) * HD)
        raw = q_ref[:, span].astype(f32)
        inv = lax.rsqrt(jnp.mean(raw * raw, axis=-1, keepdims=True) + norm_eps)
        normed = raw * inv * gain
        qt[0, :, span] = normed.T.astype(bf16)

    rest = slice(own_grads * CHUNK, padded)
    dkt[:, rest] = jnp.zeros_like(dkt[:, rest])
    dvt[:, rest] = jnp.zeros_like(dvt[:, rest])
    pl.semaphore_wait(barrier, 5)

    @pl.when(has_left)
    def _():
        q_copy.start()

    for h in range(heads):
        span = slice(h * HD, (h + 1) * HD)
        gt[0, :, span] = g_ref[:, span].T
    for copy in row_copies:
        copy.wait()
    first_key = key_rows_ref[0:1, :]

    def fill(start, rows, key_rows, value_rows):
        held = key_rows.shape[0]
        at = start + lax.broadcasted_iota(jnp.int32, (rows, HD), 0)
        if held < rows:
            pad = jnp.zeros((rows - held, HD), bf16)
            key_rows = jnp.concatenate([key_rows, pad], axis=0)
            value_rows = jnp.concatenate([value_rows, pad], axis=0)
        live = at < limit
        key_f = key_rows.astype(f32)
        value_low = jnp.where(live, value_rows.astype(f32), 0.0).astype(bf16)
        keys[pl.ds(start, rows), :] = jnp.where(live, key_f, first_key.astype(f32)).astype(bf16)
        values[pl.ds(start, rows), :] = value_low
        keys_t[:, pl.ds(start, rows)] = jnp.where(live, key_f, 0.0).astype(bf16).T
        values_t[0:HD, pl.ds(start, rows)] = value_low.T
        live_t = start + lax.broadcasted_iota(jnp.int32, (16, rows), 1) < limit
        values_t[HD : HD + 16, pl.ds(start, rows)] = jnp.where(live_t, 1.0, 0.0).astype(bf16)

    def fill_chunk(i):
        start = pl.multiple_of(i * CHUNK, CHUNK)
        span = pl.ds(start, CHUNK)
        fill(start, CHUNK, key_rows_ref[span, :], value_rows_ref[span, :])

    whole = key_count // CHUNK
    if whole < chunks:
        tail = whole * CHUNK
        fill(tail, CHUNK, key_rows_ref[tail:key_count, :], value_rows_ref[tail:key_count, :])
    fill_chunk(0)
    fill_chunk(1)

    def columns(j):
        return slice(j * GROUP, (j + 1) * GROUP)

    def chunk_start(i):
        return pl.multiple_of(i * CHUNK, CHUNK)

    def totals_pass(b, stats, low_chunk, high_chunk, fills=0):
        def scores_of(start, j):
            return nn(keys[pl.ds(start, CHUNK), :], qt[b, :, columns(j)])

        for j in range(groups):
            span = columns(j)
            first = scores_of(low_chunk * CHUNK, j)
            held[:, span] = first
            top = jnp.max(first, axis=0, keepdims=True) * exp2_scale
            if low_chunk == 0:
                stats[0:1, span] = top
                stats[1:2, span] = top
            else:
                before = stats[0:1, span]
                stats[0:1, span] = jnp.maximum(before, top)
                stats[1:2, span] = before
        if low_chunk == 0:
            acc[b] = jnp.zeros(acc.shape[1:], f32)

        def step(i, carry, last=False, fill=False):
            start = chunk_start(i)
            value_chunk = values_t[:, pl.ds(start, CHUNK)]
            if fill:
                fill_chunk(2 * i + 2)
                fill_chunk(2 * i + 3)
            for j in range(groups):
                span = columns(j)
                top = stats[0:1, span]
                before = stats[1:2, span]
                low = jnp.exp2(held[:, span] * exp2_scale - top).astype(bf16)
                m_all[b, i, 0:1, span] = top
                e_all[b, pl.ds(start, CHUNK), span] = low
                if not last:
                    later = scores_of(chunk_start(i + 1), j)
                    held[:, span] = later
                    stats[0:1, span] = jnp.maximum(
                        top, jnp.max(later, axis=0, keepdims=True) * exp2_scale
                    )
                    stats[1:2, span] = top
                acc[b, :, span] = acc[b, :, span] * jnp.exp2(before - top) + nn(value_chunk, low)
            return carry

        if fills:
            lax.fori_loop(low_chunk, fills, functools.partial(step, fill=True), 0)
        lax.fori_loop(max(low_chunk, fills), high_chunk - 1, step, 0)
        step(high_chunk - 1, 0, last=True)

    def finish_totals(b, stats):
        stats[1:2, :] = acc[b, HD : HD + 1, :]
        stats[2:3, :] = jnp.sum(acc[b, 0:HD, :] * gt[b].astype(f32), axis=0, keepdims=True)

    totals_pass(0, stats_own, 0, own_totals, fills=(whole - 2) // 2)

    @pl.when(has_left)
    def _():
        g_copy.start()

    @pl.when(has_next)
    def _():
        q_copy.wait_recv()
        totals_pass(1, stats_send, 0, chunks)
        g_copy.wait_recv()
        finish_totals(1, stats_send)
        stats_copy.start()

    totals_pass(0, stats_own, own_totals, chunks)
    finish_totals(0, stats_own)

    @pl.when(has_left)
    def _():
        stats_copy.wait_recv()
        m1, l1, d1 = stats_own[0:1, :], stats_own[1:2, :], stats_own[2:3, :]
        m2, l2, d2 = stats_in[0:1, :], stats_in[1:2, :], stats_in[2:3, :]
        top = jnp.maximum(m1, m2)
        w1, w2 = jnp.exp2(m1 - top), jnp.exp2(m2 - top)
        norm = l1 * w1 + l2 * w2
        total[0, 0:1, :] = top + jnp.log2(norm)
        total[0, 1:2, :] = (d1 * w1 + d2 * w2) / norm
        total_copy.start()

    @pl.when(jnp.logical_not(has_left))
    def _():
        norm = stats_own[1:2, :]
        total[0, 0:1, :] = stats_own[0:1, :] + jnp.log2(norm)
        total[0, 1:2, :] = stats_own[2:3, :] / norm

    def grads_pass(b, totals, write, low_chunk, high_chunk):
        def slopes_of(start, j):
            return nn(values[pl.ds(start, CHUNK), :], gt[b, :, columns(j)])

        for j in range(groups):
            held[:, columns(j)] = slopes_of(low_chunk * CHUNK, j)
        if low_chunk == 0:
            dqt[b] = jnp.zeros(dqt.shape[1:], f32)

        def step(i, carry, last=False):
            start = chunk_start(i)
            key_chunk = keys_t[:, pl.ds(start, CHUNK)]
            key_part, value_part = None, None
            for j in range(groups):
                span = columns(j)
                weight = jnp.exp2(m_all[b, i, 0:1, span] - totals[0:1, span])
                probs = e_all[b, pl.ds(start, CHUNK), span].astype(f32) * weight
                probs_low = probs.astype(bf16)
                score_grad = (probs * (held[:, span] - totals[1:2, span])).astype(bf16)
                if not last:
                    held[:, span] = slopes_of(chunk_start(i + 1), j)
                probs_t[span, :] = probs_low.T
                grads_t[span, :] = score_grad.T
                v_part = nn(gt[b, :, span], probs_t[span, :])
                k_part = nn(qt[b, :, span], grads_t[span, :])
                dqt[b, :, span] += nn(key_chunk, score_grad)
                key_part = k_part if j == 0 else key_part + k_part
                value_part = v_part if j == 0 else value_part + v_part
            write(start, key_part, value_part)
            return carry

        lax.fori_loop(low_chunk, high_chunk - 1, step, 0)
        step(high_chunk - 1, 0, True)

    def hold(start, key_part, value_part):
        dkt[:, pl.ds(start, CHUNK)] = key_part
        dvt[:, pl.ds(start, CHUNK)] = value_part

    def emit(start, key_part, value_part):
        hold(start, key_part + dkt[:, pl.ds(start, CHUNK)], value_part + dvt[:, pl.ds(start, CHUNK)])

    grads_pass(0, total.at[0], hold, 0, own_grads)

    @pl.when(has_next)
    def _():
        total_copy.wait_recv()
        grads_pass(1, total_in, emit, 0, chunks)
        dq_send[...] = dqt[1].astype(bf16)
        dq_copy.start()

    weight_copies[0].start()
    grads_pass(0, total.at[0], emit, own_grads, chunks)

    def output(i):
        start = i * CHUNK
        rows = min(CHUNK, key_count - start)
        live = start + lax.broadcasted_iota(jnp.int32, (rows, HD), 0) < limit
        span = slice(start, start + CHUNK)
        key_rows = (dkt[:, span] * score_scale).T[0:rows]
        value_rows = dvt[:, span].T[0:rows]
        key_rows_ref[start : start + rows, :] = jnp.where(live, key_rows, 0.0).astype(bf16)
        value_rows_ref[start : start + rows, :] = jnp.where(live, value_rows, 0.0).astype(bf16)
        if i == chunks - 1:
            for copy in out_copies:
                copy.start()

    @pl.when(has_left)
    def _():
        dq_copy.wait_recv()
        dqt[0] += dq_in[...].astype(f32)

    for h in range(heads):
        span = slice(h * HD, (h + 1) * HD)
        raw = q_ref[:, span].astype(f32)
        inv = lax.rsqrt(jnp.mean(raw * raw, axis=-1, keepdims=True) + norm_eps)
        scaled = dqt[0, :, span].T * score_scale * gain
        spread = jnp.mean(scaled * raw, axis=-1, keepdims=True)
        raw_low[:, span] = (inv * scaled - raw * (inv * inv * inv) * spread).astype(bf16)

    half = width // 2

    def part_copy(kind, n, src, dst, device):
        return pltpu.make_async_remote_copy(
            src_ref=src,
            dst_ref=dst,
            send_sem=part_send_sem.at[kind, n],
            recv_sem=part_recv_sem.at[kind, n],
            device_id=device,
            device_id_type=MESH,
        )

    def pair_copy(n):
        return part_copy(0, n, pair_send.at[n], pair_in.at[n], pair)

    def far_copies(n):
        return (
            part_copy(1, n, far_send.at[0, n], far_in.at[0, n], up),
            part_copy(2, n, far_send.at[1, n], far_in.at[1, n], down),
        )

    def near_copies(n):
        return (
            part_copy(3, n, near_send.at[0, n], near_in.at[0, n], up),
            part_copy(4, n, near_send.at[1, n], near_in.at[1, n], down),
        )

    def kept(n, place):
        return pl.ds(pl.multiple_of((n * chips + place) * 16, 16), 16)

    def multiply(n):
        if (n + 1) * width <= early:
            rows = e_all[1, n * width : (n + 1) * width, :]
        else:
            rows = weight_tail[n * width - early : (n + 1) * width - early, :]
        product = nt(raw_low[...], rows).reshape(chips, 2, 16, width)
        first, second = product[:, 0], product[:, 1]
        held[n * chips * 16 : (n + 1) * chips * 16, :] = jnp.where(
            core == 0, first, second
        ).reshape(chips * 16, width)
        pair_send[n] = jnp.where(core == 0, second, first).astype(bf16)
        pair_copy(n).start()

    def send_far(n):
        pair_copy(n).wait_recv()
        held[n * chips * 16 : (n + 1) * chips * 16, :] += (
            pair_in[n].astype(f32).reshape(chips * 16, width)
        )
        far = held[kept(n, far_chip), :].astype(bf16)
        far_send[0, n] = far[:, 0:half]
        far_send[1, n] = far[:, half:width]
        for copy in far_copies(n):
            copy.start()

    def send_near(n):
        for copy in far_copies(n):
            copy.wait_recv()
        one, other = held[kept(n, up_chip), :], held[kept(n, down_chip), :]
        near_send[0, n, :, 0:half] = (one[:, 0:half] + far_in[0, n].astype(f32)).astype(bf16)
        near_send[0, n, :, half:width] = one[:, half:width].astype(bf16)
        near_send[1, n, :, 0:half] = other[:, 0:half].astype(bf16)
        near_send[1, n, :, half:width] = (other[:, half:width] + far_in[1, n].astype(f32)).astype(bf16)
        for copy in near_copies(n):
            copy.start()

    def finish(n):
        for copy in near_copies(n):
            copy.wait_recv()
        whole_sum = held[kept(n, chip), :] + near_in[0, n].astype(f32) + near_in[1, n].astype(f32)
        text_out[:, n * width : (n + 1) * width] = whole_sum.astype(bf16)

    for copy in weight_copies:
        copy.wait()
    for t in range(PARTS + 10):
        for lag, stage in ((0, multiply), (3, send_far), (6, send_near), (10, finish)):
            if 0 <= t - lag < PARTS:
                stage(t - lag)
        if 3 <= t < chunks + 3:
            output(t - 3)
    for copy in out_copies:
        copy.wait()
    for n in range(PARTS):
        for copy in (pair_copy(n), *far_copies(n), *near_copies(n)):
            copy.wait_send()

    @pl.when(has_left)
    def _():
        q_copy.wait_send()
        g_copy.wait_send()
        total_copy.wait_send()

    @pl.when(has_next)
    def _():
        stats_copy.wait_send()
        dq_copy.wait_send()


def hand_over_kernel(
    text_in, key_in, value_in, text_out, key_out, value_out, text, keys, values, in_sem, out_sem
):
    held = (text, keys, values)
    arrive = [
        pltpu.make_async_copy(src, dst, in_sem.at[n])
        for n, (src, dst) in enumerate(zip((text_in, key_in, value_in), held))
    ]
    leave = [
        pltpu.make_async_copy(src, dst, out_sem.at[n])
        for n, (src, dst) in enumerate(zip(held, (text_out, key_out, value_out)))
    ]
    for copy in arrive:
        copy.start()
    for first, second in zip(arrive, leave):
        first.wait()
        second.start()
    for copy in leave:
        copy.wait()


def on_device(
    q_raw,
    out_grad,
    q_gain,
    image_keys,
    image_values,
    block_images,
    image_slot,
    tile_counts,
    q_weight,
):
    rows, cols = q_raw.shape
    key_count = image_keys.shape[1]
    padded = -(-key_count // CHUNK) * CHUNK
    chunks = padded // CHUNK
    smem = pl.BlockSpec(memory_space=pltpu.SMEM)
    vmem = pl.BlockSpec(memory_space=pltpu.VMEM)
    hbm = pl.BlockSpec(memory_space=pl.ANY)
    V = pltpu.VMEM
    width = q_weight.shape[0] // PARTS
    weight_rest = q_weight.shape[0] - padded // width * width
    chips = lax.axis_size("tp") // 2
    results = pl.pallas_call(
        attention_kernel,
        out_shape=(
            jax.ShapeDtypeStruct((rows // (2 * chips), q_weight.shape[0]), bf16),
            jax.ShapeDtypeStruct(image_keys.shape, bf16),
            jax.ShapeDtypeStruct(image_values.shape, bf16),
        ),
        in_specs=[smem] * 2 + [vmem] * 3 + [hbm] * 3,
        out_specs=(vmem, hbm, hbm),
        scratch_shapes=[
            V((key_count, HD), bf16),
            V((key_count, HD), bf16),
            V((padded, HD), bf16),
            V((padded, HD), bf16),
            V((HD, padded), bf16),
            V((HD + 16, padded), bf16),
            V((2, HD, cols), bf16),
            V((2, HD, cols), bf16),
            V((2, padded, cols), bf16),
            V((2, chunks, 1, cols), f32),
            V((CHUNK, cols), f32),
            V((cols, CHUNK), bf16),
            V((cols, CHUNK), bf16),
            V((2, HD + 16, cols), f32),
            V((HD, padded), f32),
            V((HD, padded), f32),
            V((2, HD, cols), f32),
            V((8, cols), f32),
            V((8, cols), f32),
            V((8, cols), f32),
            V((1, 8, cols), f32),
            V((8, cols), f32),
            V((HD, cols), bf16),
            V((HD, cols), bf16),
            V((rows, cols), bf16),
            V((weight_rest, cols), bf16),
            V((PARTS, chips, 16, width), bf16),
            V((PARTS, chips, 16, width), bf16),
            V((2, PARTS, 16, width // 2), bf16),
            V((2, PARTS, 16, width // 2), bf16),
            V((2, PARTS, 16, width), bf16),
            V((2, PARTS, 16, width), bf16),
            pltpu.SemaphoreType.DMA((6,)),
            pltpu.SemaphoreType.DMA((5,)),
            pltpu.SemaphoreType.DMA((5,)),
            pltpu.SemaphoreType.DMA((5, PARTS)),
            pltpu.SemaphoreType.DMA((5, PARTS)),
        ],
        compiler_params=pltpu.CompilerParams(
            collective_id=0, has_side_effects=True, vmem_limit_bytes=63 << 20
        ),
        name="attention",
    )(image_slot, tile_counts, q_raw, out_grad, q_gain.reshape(1, HD), image_keys, image_values, q_weight)
    return pl.pallas_call(
        hand_over_kernel,
        out_shape=tuple(jax.ShapeDtypeStruct(x.shape, x.dtype) for x in results),
        in_specs=[hbm] * 3,
        out_specs=(hbm, hbm, hbm),
        scratch_shapes=[V(x.shape, x.dtype) for x in results]
        + [pltpu.SemaphoreType.DMA((3,))] * 2,
        compiler_params=pltpu.CompilerParams(vmem_limit_bytes=63 << 20),
        name="hand_over",
    )(*results)


def solution(mesh):
    return jax.shard_map(
        on_device,
        mesh=mesh,
        in_specs=(
            P("seq", "tp"),
            P("seq", "tp"),
            P(),
            P("seq", None, "tp"),
            P("seq", None, "tp"),
            P(),
            P(),
            P(),
            P(None, "tp"),
        ),
        out_specs=(P(("seq", "tp"), None), P("seq", None, "tp"), P("seq", None, "tp")),
        check_vma=False,
    )
```

```python
import functools
import math

import jax
import jax.numpy as jnp
from jax import lax
from jax.experimental import pallas as pl
from jax.experimental.pallas import tpu as pltpu
from jax.sharding import PartitionSpec as P

HD = 128
TILE_TOK = 1601
CHUNK = 512
GROUP = 256
PARTS = 8
UNROLL = 4
norm_eps = 1e-05
score_scale = 1.0 / math.sqrt(HD)
exp2_scale = score_scale * math.log2(math.e)
MESH = pl.DeviceIdType.MESH
bf16, f32 = jnp.bfloat16, jnp.float32


def nn(a, b):
    return jnp.dot(a, b, preferred_element_type=f32)


def nt(a, b):
    return lax.dot_general(a, b, (((1,), (1,)), ((), ())), preferred_element_type=f32)


def run_chunks(unroll, low, high, step):
    trips = (high - low) // unroll

    def body(k, carry):
        for u in range(unroll):
            step(low + k * unroll + u, 0)
        return carry

    lax.fori_loop(0, trips, body, 0)
    for i in range(low + trips * unroll, high):
        step(i, 0)


def attention_kernel(
    slot_ref,
    tiles_ref,
    q_ref,
    g_ref,
    gain_ref,
    key_ref,
    value_ref,
    weight_ref,
    text_out,
    key_out,
    value_out,
    key_rows_ref,
    value_rows_ref,
    keys,
    values,
    keys_t,
    values_t,
    qt,
    gt,
    e_all,
    m_all,
    held,
    probs_t,
    grads_t,
    acc,
    dkt,
    dvt,
    dqt,
    stats_own,
    stats_send,
    stats_in,
    total,
    total_in,
    dq_send,
    dq_in,
    raw_low,
    weight_tail,
    pair_send,
    pair_in,
    far_send,
    far_in,
    near_send,
    near_in,
    local_sem,
    send_sem,
    recv_sem,
    part_send_sem,
    part_recv_sem,
):
    seq = lax.axis_index("seq")
    tp = lax.axis_index("tp")
    seq_size = lax.axis_size("seq")
    has_left = seq > 0
    has_next = seq < seq_size - 1
    left = (jnp.maximum(seq - 1, 0), tp)
    right = (jnp.minimum(seq + 1, seq_size - 1), tp)
    heads = q_ref.shape[1] // HD
    cols = q_ref.shape[1]
    key_count = key_ref.shape[1]
    padded = keys.shape[0]
    chunks = padded // CHUNK
    groups = cols // GROUP
    own_totals = chunks * 2 // 3
    own_grads = chunks // 4
    limit = jnp.int32(0)
    for i in range(slot_ref.shape[0]):
        limit += jnp.where(slot_ref[i] == seq, tiles_ref[i], 0)
    limit = limit * TILE_TOK

    barrier = pltpu.get_barrier_semaphore()

    chips = lax.axis_size("tp") // 2
    chip, core = lax.div(tp, 2), lax.rem(tp, 2)
    pair = (seq, tp + 1 - 2 * core)
    up_chip, down_chip = lax.rem(chip + 1, chips), lax.rem(chip + chips - 1, chips)
    far_chip = lax.rem(chip + 2, chips)
    up, down = (seq, up_chip * 2 + core), (seq, down_chip * 2 + core)
    ahead, behind = lax.rem(seq + 1, seq_size), lax.rem(seq + seq_size - 1, seq_size)
    for near in ((ahead, tp), (behind, tp), pair, up, down):
        pl.semaphore_signal(barrier, inc=1, device_id=near, device_id_type=MESH)

    def rdma(index, src, dst, device):
        return pltpu.make_async_remote_copy(
            src_ref=src,
            dst_ref=dst,
            send_sem=send_sem.at[index],
            recv_sem=recv_sem.at[index],
            device_id=device,
            device_id_type=MESH,
        )

    q_copy = rdma(0, qt.at[0], qt.at[1], left)
    g_copy = rdma(1, gt.at[0], gt.at[1], left)
    stats_copy = rdma(2, stats_send, stats_in, right)
    total_copy = rdma(3, total.at[0], total_in, left)
    dq_copy = rdma(4, dq_send, dq_in, right)

    width = weight_ref.shape[0] // PARTS
    early = (padded // width) * width
    weight_copies = (
        pltpu.make_async_copy(
            weight_ref.at[0:early], e_all.at[1, 0:early], local_sem.at[0]
        ),
        pltpu.make_async_copy(weight_ref.at[early:], weight_tail, local_sem.at[1]),
    )
    row_copies = (
        pltpu.make_async_copy(key_ref.at[0], key_rows_ref, local_sem.at[2]),
        pltpu.make_async_copy(value_ref.at[0], value_rows_ref, local_sem.at[3]),
    )
    out_copies = (
        pltpu.make_async_copy(key_rows_ref, key_out.at[0], local_sem.at[4]),
        pltpu.make_async_copy(value_rows_ref, value_out.at[0], local_sem.at[5]),
    )
    for copy in row_copies:
        copy.start()
    weight_copies[1].start()

    gain = gain_ref[...]
    for h in range(heads):
        span = slice(h * HD, (h + 1) * HD)
        raw = q_ref[:, span].astype(f32)
        inv = lax.rsqrt(jnp.mean(raw * raw, axis=-1, keepdims=True) + norm_eps)
        normed = raw * inv * gain
        qt[0, :, span] = normed.T.astype(bf16)

    pl.semaphore_wait(barrier, 5)

    @pl.when(has_left)
    def _():
        q_copy.start()

    for copy in row_copies:
        copy.wait()
    first_key = key_rows_ref[0:1, :]

    def fill(start, rows, key_rows, value_rows):
        held = key_rows.shape[0]
        at = start + lax.broadcasted_iota(jnp.int32, (rows, HD), 0)
        if held < rows:
            pad = jnp.zeros((rows - held, HD), bf16)
            key_rows = jnp.concatenate([key_rows, pad], axis=0)
            value_rows = jnp.concatenate([value_rows, pad], axis=0)
        live = at < limit
        key_f = key_rows.astype(f32)
        value_low = jnp.where(live, value_rows.astype(f32), 0.0).astype(bf16)
        keys[pl.ds(start, rows), :] = jnp.where(live, key_f, first_key.astype(f32)).astype(bf16)
        values[pl.ds(start, rows), :] = value_low
        keys_t[:, pl.ds(start, rows)] = jnp.where(live, key_f, 0.0).astype(bf16).T
        values_t[0:HD, pl.ds(start, rows)] = value_low.T
        live_t = start + lax.broadcasted_iota(jnp.int32, (16, rows), 1) < limit
        values_t[HD : HD + 16, pl.ds(start, rows)] = jnp.where(live_t, 1.0, 0.0).astype(bf16)

    def fill_chunk(i):
        start = pl.multiple_of(i * CHUNK, CHUNK)
        span = pl.ds(start, CHUNK)
        fill(start, CHUNK, key_rows_ref[span, :], value_rows_ref[span, :])

    whole = key_count // CHUNK
    if whole < chunks:
        tail = whole * CHUNK
        fill(tail, CHUNK, key_rows_ref[tail:key_count, :], value_rows_ref[tail:key_count, :])
    fill_chunk(0)
    fill_chunk(1)

    def columns(j):
        return slice(j * GROUP, (j + 1) * GROUP)

    def chunk_start(i):
        return pl.multiple_of(i * CHUNK, CHUNK)

    def totals_pass(b, stats, low_chunk, high_chunk, fills=0):
        def scores_of(start, j):
            return nn(keys[pl.ds(start, CHUNK), :], qt[b, :, columns(j)])

        for j in range(groups):
            span = columns(j)
            first = scores_of(low_chunk * CHUNK, j)
            held[:, span] = first
            top = jnp.max(first, axis=0, keepdims=True) * exp2_scale
            if low_chunk == 0:
                stats[0:1, span] = top
                stats[1:2, span] = top
            else:
                before = stats[0:1, span]
                stats[0:1, span] = jnp.maximum(before, top)
                stats[1:2, span] = before
        if low_chunk == 0:
            acc[b] = jnp.zeros(acc.shape[1:], f32)

        def step(i, carry, last=False, fill=False):
            start = chunk_start(i)
            value_chunk = values_t[:, pl.ds(start, CHUNK)]
            if fill:
                fill_chunk(2 * i + 2)
                fill_chunk(2 * i + 3)
            for j in range(groups):
                span = columns(j)
                top = stats[0:1, span]
                before = stats[1:2, span]
                low = jnp.exp2(held[:, span] * exp2_scale - top).astype(bf16)
                m_all[b, i, 0:1, span] = top
                e_all[b, pl.ds(start, CHUNK), span] = low
                if not last:
                    later = scores_of(chunk_start(i + 1), j)
                    held[:, span] = later
                    stats[0:1, span] = jnp.maximum(
                        top, jnp.max(later, axis=0, keepdims=True) * exp2_scale
                    )
                    stats[1:2, span] = top
                acc[b, :, span] = acc[b, :, span] * jnp.exp2(before - top) + nn(value_chunk, low)
            return carry

        if fills:
            run_chunks(1, low_chunk, fills, functools.partial(step, fill=True))
        run_chunks(UNROLL, max(low_chunk, fills), high_chunk - 1, step)
        step(high_chunk - 1, 0, last=True)

    def finish_totals(b, stats):
        stats[1:2, :] = acc[b, HD : HD + 1, :]
        stats[2:3, :] = jnp.sum(acc[b, 0:HD, :] * gt[b].astype(f32), axis=0, keepdims=True)

    totals_pass(0, stats_own, 0, own_totals, fills=(whole - 2) // 2)
    for h in range(heads):
        span = slice(h * HD, (h + 1) * HD)
        gt[0, :, span] = g_ref[:, span].T
    rest = slice(own_grads * CHUNK, padded)
    dkt[:, rest] = jnp.zeros_like(dkt[:, rest])
    dvt[...] = jnp.zeros_like(dvt)

    @pl.when(has_left)
    def _():
        g_copy.start()

    @pl.when(has_next)
    def _():
        q_copy.wait_recv()
        totals_pass(1, stats_send, 0, chunks)
        g_copy.wait_recv()
        finish_totals(1, stats_send)
        stats_copy.start()

    totals_pass(0, stats_own, own_totals, chunks)
    finish_totals(0, stats_own)

    @pl.when(has_left)
    def _():
        stats_copy.wait_recv()
        m1, l1, d1 = stats_own[0:1, :], stats_own[1:2, :], stats_own[2:3, :]
        m2, l2, d2 = stats_in[0:1, :], stats_in[1:2, :], stats_in[2:3, :]
        top = jnp.maximum(m1, m2)
        w1, w2 = jnp.exp2(m1 - top), jnp.exp2(m2 - top)
        norm = l1 * w1 + l2 * w2
        total[0, 0:1, :] = top + jnp.log2(norm)
        total[0, 1:2, :] = (d1 * w1 + d2 * w2) / norm
        total_copy.start()

    @pl.when(jnp.logical_not(has_left))
    def _():
        norm = stats_own[1:2, :]
        total[0, 0:1, :] = stats_own[0:1, :] + jnp.log2(norm)
        total[0, 1:2, :] = stats_own[2:3, :] / norm

    def grads_pass(b, totals, write, low_chunk, high_chunk):
        def slopes_of(start, j):
            return nn(values[pl.ds(start, CHUNK), :], gt[b, :, columns(j)])

        for j in range(groups):
            held[:, columns(j)] = slopes_of(low_chunk * CHUNK, j)
        if low_chunk == 0:
            dqt[b] = jnp.zeros(dqt.shape[1:], f32)

        def step(i, carry, last=False):
            start = chunk_start(i)
            key_chunk = keys_t[:, pl.ds(start, CHUNK)]
            key_part, value_part = None, None
            for j in range(groups):
                span = columns(j)
                weight = jnp.exp2(m_all[b, i, 0:1, span] - totals[0:1, span])
                probs = e_all[b, pl.ds(start, CHUNK), span].astype(f32) * weight
                probs_low = probs.astype(bf16)
                score_grad = (probs * (held[:, span] - totals[1:2, span])).astype(bf16)
                if not last:
                    held[:, span] = slopes_of(chunk_start(i + 1), j)
                if b == 0:
                    e_all[b, pl.ds(start, CHUNK), span] = probs_low
                else:
                    probs_t[span, :] = probs_low.T
                grads_t[span, :] = score_grad.T
                k_part = nn(qt[b, :, span], grads_t[span, :])
                dqt[b, :, span] += nn(key_chunk, score_grad)
                key_part = k_part if j == 0 else key_part + k_part
                if b > 0:
                    v_part = nn(gt[b, :, span], probs_t[span, :])
                    value_part = v_part if j == 0 else value_part + v_part
            write(start, key_part, value_part)
            return carry

        run_chunks(UNROLL, low_chunk, high_chunk - 1, step)
        step(high_chunk - 1, 0, True)

    def hold(start, key_part, value_part):
        dkt[:, pl.ds(start, CHUNK)] = key_part

    def emit(start, key_part, value_part):
        dkt[:, pl.ds(start, CHUNK)] += key_part
        if value_part is not None:
            dvt[:, pl.ds(start, CHUNK)] += value_part

    grads_pass(0, total.at[0], hold, 0, own_grads)

    @pl.when(has_next)
    def _():
        total_copy.wait_recv()
        grads_pass(1, total_in, emit, 0, chunks)
        dq_send[...] = dqt[1].astype(bf16)
        dq_copy.start()

    weight_copies[0].start()
    grads_pass(0, total.at[0], emit, own_grads, chunks)

    def output(i):
        start = i * CHUNK
        rows = min(CHUNK, key_count - start)
        live = start + lax.broadcasted_iota(jnp.int32, (rows, HD), 0) < limit
        span = slice(start, start + CHUNK)
        key_rows = (dkt[:, span] * score_scale).T[0:rows]
        value_rows = (dvt[:, span] + nt(gt[0], e_all[0, span, :])).T[0:rows]
        key_rows_ref[start : start + rows, :] = jnp.where(live, key_rows, 0.0).astype(bf16)
        value_rows_ref[start : start + rows, :] = jnp.where(live, value_rows, 0.0).astype(bf16)
        if i == chunks - 1:
            for copy in out_copies:
                copy.start()

    @pl.when(has_left)
    def _():
        dq_copy.wait_recv()
        dqt[0] += dq_in[...].astype(f32)

    for h in range(heads):
        span = slice(h * HD, (h + 1) * HD)
        raw = q_ref[:, span].astype(f32)
        inv = lax.rsqrt(jnp.mean(raw * raw, axis=-1, keepdims=True) + norm_eps)
        scaled = dqt[0, :, span].T * score_scale * gain
        spread = jnp.mean(scaled * raw, axis=-1, keepdims=True)
        raw_low[:, span] = (inv * scaled - raw * (inv * inv * inv) * spread).astype(bf16)

    half = width // 2

    def part_copy(kind, n, src, dst, device):
        return pltpu.make_async_remote_copy(
            src_ref=src,
            dst_ref=dst,
            send_sem=part_send_sem.at[kind, n],
            recv_sem=part_recv_sem.at[kind, n],
            device_id=device,
            device_id_type=MESH,
        )

    def pair_copy(n):
        return part_copy(0, n, pair_send.at[n], pair_in.at[n], pair)

    def far_copies(n):
        return (
            part_copy(1, n, far_send.at[0, n], far_in.at[0, n], up),
            part_copy(2, n, far_send.at[1, n], far_in.at[1, n], down),
        )

    def near_copies(n):
        return (
            part_copy(3, n, near_send.at[0, n], near_in.at[0, n], up),
            part_copy(4, n, near_send.at[1, n], near_in.at[1, n], down),
        )

    def kept(n, place):
        return pl.ds(pl.multiple_of((n * chips + place) * 16, 16), 16)

    def multiply(n):
        if (n + 1) * width <= early:
            rows = e_all[1, n * width : (n + 1) * width, :]
        else:
            rows = weight_tail[n * width - early : (n + 1) * width - early, :]
        product = nt(raw_low[...], rows).reshape(chips, 2, 16, width)
        first, second = product[:, 0], product[:, 1]
        held[n * chips * 16 : (n + 1) * chips * 16, :] = jnp.where(
            core == 0, first, second
        ).reshape(chips * 16, width)
        pair_send[n] = jnp.where(core == 0, second, first).astype(bf16)
        pair_copy(n).start()

    def send_far(n):
        pair_copy(n).wait_recv()
        held[n * chips * 16 : (n + 1) * chips * 16, :] += (
            pair_in[n].astype(f32).reshape(chips * 16, width)
        )
        far = held[kept(n, far_chip), :].astype(bf16)
        far_send[0, n] = far[:, 0:half]
        far_send[1, n] = far[:, half:width]
        for copy in far_copies(n):
            copy.start()

    def send_near(n):
        for copy in far_copies(n):
            copy.wait_recv()
        one, other = held[kept(n, up_chip), :], held[kept(n, down_chip), :]
        near_send[0, n, :, 0:half] = (one[:, 0:half] + far_in[0, n].astype(f32)).astype(bf16)
        near_send[0, n, :, half:width] = one[:, half:width].astype(bf16)
        near_send[1, n, :, 0:half] = other[:, 0:half].astype(bf16)
        near_send[1, n, :, half:width] = (other[:, half:width] + far_in[1, n].astype(f32)).astype(bf16)
        for copy in near_copies(n):
            copy.start()

    def finish(n):
        for copy in near_copies(n):
            copy.wait_recv()
        whole_sum = held[kept(n, chip), :] + near_in[0, n].astype(f32) + near_in[1, n].astype(f32)
        text_out[:, n * width : (n + 1) * width] = whole_sum.astype(bf16)

    for copy in weight_copies:
        copy.wait()
    for t in range(PARTS + 10):
        for lag, stage in ((0, multiply), (3, send_far), (6, send_near), (10, finish)):
            if 0 <= t - lag < PARTS:
                stage(t - lag)
        if 3 <= t < chunks + 3:
            output(t - 3)
    for copy in out_copies:
        copy.wait()
    for n in range(PARTS):
        for copy in (pair_copy(n), *far_copies(n), *near_copies(n)):
            copy.wait_send()

    @pl.when(has_left)
    def _():
        q_copy.wait_send()
        g_copy.wait_send()
        total_copy.wait_send()

    @pl.when(has_next)
    def _():
        stats_copy.wait_send()
        dq_copy.wait_send()


def hand_over_kernel(
    text_in, key_in, value_in, text_out, key_out, value_out, text, keys, values, in_sem, out_sem
):
    held = (text, keys, values)
    arrive = [
        pltpu.make_async_copy(src, dst, in_sem.at[n])
        for n, (src, dst) in enumerate(zip((text_in, key_in, value_in), held))
    ]
    leave = [
        pltpu.make_async_copy(src, dst, out_sem.at[n])
        for n, (src, dst) in enumerate(zip(held, (text_out, key_out, value_out)))
    ]
    for copy in arrive:
        copy.start()
    for first, second in zip(arrive, leave):
        first.wait()
        second.start()
    for copy in leave:
        copy.wait()


def on_device(
    q_raw,
    out_grad,
    q_gain,
    image_keys,
    image_values,
    block_images,
    image_slot,
    tile_counts,
    q_weight,
):
    rows, cols = q_raw.shape
    key_count = image_keys.shape[1]
    padded = -(-key_count // CHUNK) * CHUNK
    chunks = padded // CHUNK
    smem = pl.BlockSpec(memory_space=pltpu.SMEM)
    vmem = pl.BlockSpec(memory_space=pltpu.VMEM)
    hbm = pl.BlockSpec(memory_space=pl.ANY)
    V = pltpu.VMEM
    width = q_weight.shape[0] // PARTS
    weight_rest = q_weight.shape[0] - padded // width * width
    chips = lax.axis_size("tp") // 2
    results = pl.pallas_call(
        attention_kernel,
        out_shape=(
            jax.ShapeDtypeStruct((rows // (2 * chips), q_weight.shape[0]), bf16),
            jax.ShapeDtypeStruct(image_keys.shape, bf16),
            jax.ShapeDtypeStruct(image_values.shape, bf16),
        ),
        in_specs=[smem] * 2 + [vmem] * 3 + [hbm] * 3,
        out_specs=(vmem, hbm, hbm),
        scratch_shapes=[
            V((key_count, HD), bf16),
            V((key_count, HD), bf16),
            V((padded, HD), bf16),
            V((padded, HD), bf16),
            V((HD, padded), bf16),
            V((HD + 16, padded), bf16),
            V((2, HD, cols), bf16),
            V((2, HD, cols), bf16),
            V((2, padded, cols), bf16),
            V((2, chunks, 1, cols), f32),
            V((CHUNK, cols), f32),
            V((cols, CHUNK), bf16),
            V((cols, CHUNK), bf16),
            V((2, HD + 16, cols), f32),
            V((HD, padded), f32),
            V((HD, padded), f32),
            V((2, HD, cols), f32),
            V((8, cols), f32),
            V((8, cols), f32),
            V((8, cols), f32),
            V((1, 8, cols), f32),
            V((8, cols), f32),
            V((HD, cols), bf16),
            V((HD, cols), bf16),
            V((rows, cols), bf16),
            V((weight_rest, cols), bf16),
            V((PARTS, chips, 16, width), bf16),
            V((PARTS, chips, 16, width), bf16),
            V((2, PARTS, 16, width // 2), bf16),
            V((2, PARTS, 16, width // 2), bf16),
            V((2, PARTS, 16, width), bf16),
            V((2, PARTS, 16, width), bf16),
            pltpu.SemaphoreType.DMA((6,)),
            pltpu.SemaphoreType.DMA((5,)),
            pltpu.SemaphoreType.DMA((5,)),
            pltpu.SemaphoreType.DMA((5, PARTS)),
            pltpu.SemaphoreType.DMA((5, PARTS)),
        ],
        compiler_params=pltpu.CompilerParams(
            collective_id=0, has_side_effects=True, vmem_limit_bytes=255 << 18
        ),
        name="attention",
    )(image_slot, tile_counts, q_raw, out_grad, q_gain.reshape(1, HD), image_keys, image_values, q_weight)
    return pl.pallas_call(
        hand_over_kernel,
        out_shape=tuple(jax.ShapeDtypeStruct(x.shape, x.dtype) for x in results),
        in_specs=[hbm] * 3,
        out_specs=(hbm, hbm, hbm),
        scratch_shapes=[V(x.shape, x.dtype) for x in results]
        + [pltpu.SemaphoreType.DMA((3,))] * 2,
        compiler_params=pltpu.CompilerParams(vmem_limit_bytes=63 << 20),
        name="hand_over",
    )(*results)


def solution(mesh):
    return jax.shard_map(
        on_device,
        mesh=mesh,
        in_specs=(
            P("seq", "tp"),
            P("seq", "tp"),
            P(),
            P("seq", None, "tp"),
            P("seq", None, "tp"),
            P(),
            P(),
            P(),
            P(None, "tp"),
        ),
        out_specs=(P(("seq", "tp"), None), P("seq", None, "tp"), P("seq", None, "tp")),
        check_vma=False,
    )
```

```python
import functools
import math

import jax
import jax.numpy as jnp
from jax import lax
from jax.experimental import pallas as pl
from jax.experimental.pallas import tpu as pltpu
from jax.sharding import PartitionSpec as P

HD = 128
TILE_TOK = 1601
CHUNK = 512
GROUP = 256
PARTS = 8
UNROLL = 4
norm_eps = 1e-05
score_scale = 1.0 / math.sqrt(HD)
exp2_scale = score_scale * math.log2(math.e)
MESH = pl.DeviceIdType.MESH
bf16, f32 = jnp.bfloat16, jnp.float32


def nn(a, b):
    return jnp.dot(a, b, preferred_element_type=f32)


def nt(a, b):
    return lax.dot_general(a, b, (((1,), (1,)), ((), ())), preferred_element_type=f32)


def run_chunks(unroll, low, high, step):
    trips = (high - low) // unroll

    def body(k, carry):
        for u in range(unroll):
            step(low + k * unroll + u, 0)
        return carry

    lax.fori_loop(0, trips, body, 0)
    for i in range(low + trips * unroll, high):
        step(i, 0)


def attention_kernel(
    slot_ref,
    tiles_ref,
    q_ref,
    g_ref,
    gain_ref,
    key_ref,
    value_ref,
    weight_ref,
    text_out,
    key_out,
    value_out,
    key_rows_ref,
    value_rows_ref,
    keys,
    values,
    keys_t,
    values_t,
    qt,
    gt,
    e_all,
    m_all,
    held,
    probs_t,
    grads_t,
    acc,
    dkt,
    dvt,
    dqt,
    stats_own,
    stats_send,
    stats_in,
    total,
    total_in,
    dq_send,
    dq_in,
    raw_low,
    weight_tail,
    pair_send,
    pair_in,
    far_send,
    far_in,
    near_send,
    near_in,
    local_sem,
    send_sem,
    recv_sem,
    part_send_sem,
    part_recv_sem,
):
    seq = lax.axis_index("seq")
    tp = lax.axis_index("tp")
    seq_size = lax.axis_size("seq")
    has_left = seq > 0
    has_next = seq < seq_size - 1
    left = (jnp.maximum(seq - 1, 0), tp)
    right = (jnp.minimum(seq + 1, seq_size - 1), tp)
    heads = q_ref.shape[1] // HD
    cols = q_ref.shape[1]
    key_count = key_ref.shape[1]
    padded = keys.shape[0]
    chunks = padded // CHUNK
    groups = cols // GROUP
    own_totals = chunks * 2 // 3
    own_grads = chunks // 4
    limit = jnp.int32(0)
    for i in range(slot_ref.shape[0]):
        limit += jnp.where(slot_ref[i] == seq, tiles_ref[i], 0)
    limit = limit * TILE_TOK

    barrier = pltpu.get_barrier_semaphore()

    chips = lax.axis_size("tp") // 2
    chip, core = lax.div(tp, 2), lax.rem(tp, 2)
    pair = (seq, tp + 1 - 2 * core)
    up_chip, down_chip = lax.rem(chip + 1, chips), lax.rem(chip + chips - 1, chips)
    far_chip = lax.rem(chip + 2, chips)
    up, down = (seq, up_chip * 2 + core), (seq, down_chip * 2 + core)
    ahead, behind = lax.rem(seq + 1, seq_size), lax.rem(seq + seq_size - 1, seq_size)
    for near in ((ahead, tp), (behind, tp), pair, up, down):
        pl.semaphore_signal(barrier, inc=1, device_id=near, device_id_type=MESH)

    def rdma(index, src, dst, device):
        return pltpu.make_async_remote_copy(
            src_ref=src,
            dst_ref=dst,
            send_sem=send_sem.at[index],
            recv_sem=recv_sem.at[index],
            device_id=device,
            device_id_type=MESH,
        )

    q_copy = rdma(0, qt.at[0], qt.at[1], left)
    g_copy = rdma(1, gt.at[0], gt.at[1], left)
    stats_copy = rdma(2, stats_send, stats_in, right)
    total_copy = rdma(3, total.at[0], total_in, left)
    dq_copy = rdma(4, dq_send, dq_in, right)

    width = weight_ref.shape[0] // PARTS
    early = (padded // width) * width
    weight_copies = (
        pltpu.make_async_copy(
            weight_ref.at[0:early], e_all.at[1, 0:early], local_sem.at[0]
        ),
        pltpu.make_async_copy(weight_ref.at[early:], weight_tail, local_sem.at[1]),
    )
    row_copies = (
        pltpu.make_async_copy(key_ref.at[0], key_rows_ref, local_sem.at[2]),
        pltpu.make_async_copy(value_ref.at[0], value_rows_ref, local_sem.at[3]),
    )
    out_copies = (
        pltpu.make_async_copy(key_rows_ref, key_out.at[0], local_sem.at[4]),
        pltpu.make_async_copy(value_rows_ref, value_out.at[0], local_sem.at[5]),
    )
    for copy in row_copies:
        copy.start()
    weight_copies[1].start()

    gain = gain_ref[...]
    for h in range(heads):
        span = slice(h * HD, (h + 1) * HD)
        raw = q_ref[:, span].astype(f32)
        inv = lax.rsqrt(jnp.mean(raw * raw, axis=-1, keepdims=True) + norm_eps)
        normed = raw * inv * gain
        qt[0, :, span] = normed.T.astype(bf16)

    pl.semaphore_wait(barrier, 5)

    @pl.when(has_left)
    def _():
        q_copy.start()

    for copy in row_copies:
        copy.wait()
    first_key = key_rows_ref[0:1, :]

    def fill(start, rows, key_rows, value_rows):
        held = key_rows.shape[0]
        at = start + lax.broadcasted_iota(jnp.int32, (rows, HD), 0)
        if held < rows:
            pad = jnp.zeros((rows - held, HD), bf16)
            key_rows = jnp.concatenate([key_rows, pad], axis=0)
            value_rows = jnp.concatenate([value_rows, pad], axis=0)
        live = at < limit
        key_f = key_rows.astype(f32)
        value_low = jnp.where(live, value_rows.astype(f32), 0.0).astype(bf16)
        keys[pl.ds(start, rows), :] = jnp.where(live, key_f, first_key.astype(f32)).astype(bf16)
        values[pl.ds(start, rows), :] = value_low
        keys_t[:, pl.ds(start, rows)] = jnp.where(live, key_f, 0.0).astype(bf16).T
        values_t[0:HD, pl.ds(start, rows)] = value_low.T
        live_t = start + lax.broadcasted_iota(jnp.int32, (16, rows), 1) < limit
        values_t[HD : HD + 16, pl.ds(start, rows)] = jnp.where(live_t, 1.0, 0.0).astype(bf16)

    def fill_chunk(i):
        start = pl.multiple_of(i * CHUNK, CHUNK)
        span = pl.ds(start, CHUNK)
        fill(start, CHUNK, key_rows_ref[span, :], value_rows_ref[span, :])

    whole = key_count // CHUNK
    if whole < chunks:
        tail = whole * CHUNK
        fill(tail, CHUNK, key_rows_ref[tail:key_count, :], value_rows_ref[tail:key_count, :])
    fill_chunk(0)
    fill_chunk(1)

    def columns(j):
        return slice(j * GROUP, (j + 1) * GROUP)

    def chunk_start(i):
        return pl.multiple_of(i * CHUNK, CHUNK)

    def totals_pass(b, stats, low_chunk, high_chunk, fills=0):
        def scores_of(start, j):
            return nn(keys[pl.ds(start, CHUNK), :], qt[b, :, columns(j)])

        for j in range(groups):
            span = columns(j)
            first = scores_of(low_chunk * CHUNK, j)
            held[:, span] = first
            top = jnp.max(first, axis=0, keepdims=True) * exp2_scale
            if low_chunk == 0:
                stats[0:1, span] = top
                stats[1:2, span] = top
            else:
                before = stats[0:1, span]
                stats[0:1, span] = jnp.maximum(before, top)
                stats[1:2, span] = before
        if low_chunk == 0:
            acc[b] = jnp.zeros(acc.shape[1:], f32)

        def step(i, carry, last=False, fill=False):
            start = chunk_start(i)
            value_chunk = values_t[:, pl.ds(start, CHUNK)]
            if fill:
                fill_chunk(2 * i + 2)
                fill_chunk(2 * i + 3)
            for j in range(groups):
                span = columns(j)
                top = stats[0:1, span]
                before = stats[1:2, span]
                low = jnp.exp2(held[:, span] * exp2_scale - top).astype(bf16)
                m_all[b, i, 0:1, span] = top
                e_all[b, pl.ds(start, CHUNK), span] = low
                if not last:
                    later = scores_of(chunk_start(i + 1), j)
                    held[:, span] = later
                    stats[0:1, span] = jnp.maximum(
                        top, jnp.max(later, axis=0, keepdims=True) * exp2_scale
                    )
                    stats[1:2, span] = top
                acc[b, :, span] = acc[b, :, span] * jnp.exp2(before - top) + nn(value_chunk, low)
            return carry

        if fills:
            run_chunks(1, low_chunk, fills, functools.partial(step, fill=True))
        run_chunks(UNROLL, max(low_chunk, fills), high_chunk - 1, step)
        step(high_chunk - 1, 0, last=True)

    def finish_totals(b, stats):
        stats[1:2, :] = acc[b, HD : HD + 1, :]
        stats[2:3, :] = jnp.sum(acc[b, 0:HD, :] * gt[b].astype(f32), axis=0, keepdims=True)

    totals_pass(0, stats_own, 0, own_totals, fills=(whole - 2) // 2)
    for h in range(heads):
        span = slice(h * HD, (h + 1) * HD)
        gt[0, :, span] = g_ref[:, span].T
    rest = slice(own_grads * CHUNK, padded)
    dkt[:, rest] = jnp.zeros_like(dkt[:, rest])
    dvt[...] = jnp.zeros_like(dvt)

    @pl.when(has_left)
    def _():
        g_copy.start()

    @pl.when(has_next)
    def _():
        q_copy.wait_recv()
        totals_pass(1, stats_send, 0, chunks)
        g_copy.wait_recv()
        finish_totals(1, stats_send)
        stats_copy.start()

    totals_pass(0, stats_own, own_totals, chunks)
    finish_totals(0, stats_own)

    @pl.when(has_left)
    def _():
        stats_copy.wait_recv()
        m1, l1, d1 = stats_own[0:1, :], stats_own[1:2, :], stats_own[2:3, :]
        m2, l2, d2 = stats_in[0:1, :], stats_in[1:2, :], stats_in[2:3, :]
        top = jnp.maximum(m1, m2)
        w1, w2 = jnp.exp2(m1 - top), jnp.exp2(m2 - top)
        norm = l1 * w1 + l2 * w2
        total[0, 0:1, :] = top + jnp.log2(norm)
        total[0, 1:2, :] = (d1 * w1 + d2 * w2) / norm
        total_copy.start()

    @pl.when(jnp.logical_not(has_left))
    def _():
        norm = stats_own[1:2, :]
        total[0, 0:1, :] = stats_own[0:1, :] + jnp.log2(norm)
        total[0, 1:2, :] = stats_own[2:3, :] / norm

    def grads_pass(b, totals, write, low_chunk, high_chunk):
        def slopes_of(start, j):
            return nn(values[pl.ds(start, CHUNK), :], gt[b, :, columns(j)])

        for j in range(groups):
            held[:, columns(j)] = slopes_of(low_chunk * CHUNK, j)
        if low_chunk == 0:
            dqt[b] = jnp.zeros(dqt.shape[1:], f32)

        def step(i, carry, last=False):
            start = chunk_start(i)
            key_chunk = keys_t[:, pl.ds(start, CHUNK)]
            key_part, value_part = None, None
            for j in range(groups):
                span = columns(j)
                weight = jnp.exp2(m_all[b, i, 0:1, span] - totals[0:1, span])
                probs = e_all[b, pl.ds(start, CHUNK), span].astype(f32) * weight
                probs_low = probs.astype(bf16)
                score_grad = (probs * (held[:, span] - totals[1:2, span])).astype(bf16)
                if not last:
                    held[:, span] = slopes_of(chunk_start(i + 1), j)
                if b == 0:
                    e_all[b, pl.ds(start, CHUNK), span] = probs_low
                else:
                    probs_t[span, :] = probs_low.T
                grads_t[span, :] = score_grad.T
                k_part = nn(qt[b, :, span], grads_t[span, :])
                dqt[b, :, span] += nn(key_chunk, score_grad)
                key_part = k_part if j == 0 else key_part + k_part
                if b > 0:
                    v_part = nn(gt[b, :, span], probs_t[span, :])
                    value_part = v_part if j == 0 else value_part + v_part
            write(start, key_part, value_part)
            return carry

        run_chunks(UNROLL, low_chunk, high_chunk - 1, step)
        step(high_chunk - 1, 0, True)

    def hold(start, key_part, value_part):
        dkt[:, pl.ds(start, CHUNK)] = key_part

    def emit(start, key_part, value_part):
        dkt[:, pl.ds(start, CHUNK)] += key_part
        if value_part is not None:
            dvt[:, pl.ds(start, CHUNK)] += value_part

    grads_pass(0, total.at[0], hold, 0, own_grads)

    @pl.when(has_next)
    def _():
        total_copy.wait_recv()
        grads_pass(1, total_in, emit, 0, chunks)
        dq_send[...] = dqt[1].astype(bf16)
        dq_copy.start()

    weight_copies[0].start()
    grads_pass(0, total.at[0], emit, own_grads, chunks)

    def output(i):
        start = i * CHUNK
        rows = min(CHUNK, key_count - start)
        live = start + lax.broadcasted_iota(jnp.int32, (rows, HD), 0) < limit
        span = slice(start, start + CHUNK)
        key_rows = (dkt[:, span] * score_scale).T[0:rows]
        value_rows = (dvt[:, span] + nt(gt[0], e_all[0, span, :])).T[0:rows]
        key_rows_ref[start : start + rows, :] = jnp.where(live, key_rows, 0.0).astype(bf16)
        value_rows_ref[start : start + rows, :] = jnp.where(live, value_rows, 0.0).astype(bf16)
        if i == chunks - 1:
            for copy in out_copies:
                copy.start()

    @pl.when(has_left)
    def _():
        dq_copy.wait_recv()
        dqt[0] += dq_in[...].astype(f32)

    for h in range(heads):
        span = slice(h * HD, (h + 1) * HD)
        raw = q_ref[:, span].astype(f32)
        inv = lax.rsqrt(jnp.mean(raw * raw, axis=-1, keepdims=True) + norm_eps)
        scaled = dqt[0, :, span].T * score_scale * gain
        spread = jnp.mean(scaled * raw, axis=-1, keepdims=True)
        raw_low[:, span] = (inv * scaled - raw * (inv * inv * inv) * spread).astype(bf16)

    half = width // 2

    def part_copy(kind, n, src, dst, device):
        return pltpu.make_async_remote_copy(
            src_ref=src,
            dst_ref=dst,
            send_sem=part_send_sem.at[kind, n],
            recv_sem=part_recv_sem.at[kind, n],
            device_id=device,
            device_id_type=MESH,
        )

    def pair_copy(n):
        return part_copy(0, n, pair_send.at[n], pair_in.at[n], pair)

    def far_copies(n):
        return (
            part_copy(1, n, far_send.at[0, n], far_in.at[0, n], up),
            part_copy(2, n, far_send.at[1, n], far_in.at[1, n], down),
        )

    def near_copies(n):
        return (
            part_copy(3, n, near_send.at[0, n], near_in.at[0, n], up),
            part_copy(4, n, near_send.at[1, n], near_in.at[1, n], down),
        )

    def kept(n, place):
        return pl.ds(pl.multiple_of((n * chips + place) * 16, 16), 16)

    def multiply(n):
        if (n + 1) * width <= early:
            rows = e_all[1, n * width : (n + 1) * width, :]
        else:
            rows = weight_tail[n * width - early : (n + 1) * width - early, :]
        product = nt(raw_low[...], rows).reshape(chips, 2, 16, width)
        first, second = product[:, 0], product[:, 1]
        held[n * chips * 16 : (n + 1) * chips * 16, :] = jnp.where(
            core == 0, first, second
        ).reshape(chips * 16, width)
        pair_send[n] = jnp.where(core == 0, second, first).astype(bf16)
        pair_copy(n).start()

    def send_far(n):
        pair_copy(n).wait_recv()
        held[n * chips * 16 : (n + 1) * chips * 16, :] += (
            pair_in[n].astype(f32).reshape(chips * 16, width)
        )
        far = held[kept(n, far_chip), :].astype(bf16)
        far_send[0, n] = far[:, 0:half]
        far_send[1, n] = far[:, half:width]
        for copy in far_copies(n):
            copy.start()

    def send_near(n):
        for copy in far_copies(n):
            copy.wait_recv()
        one, other = held[kept(n, up_chip), :], held[kept(n, down_chip), :]
        near_send[0, n, :, 0:half] = (one[:, 0:half] + far_in[0, n].astype(f32)).astype(bf16)
        near_send[0, n, :, half:width] = one[:, half:width].astype(bf16)
        near_send[1, n, :, 0:half] = other[:, 0:half].astype(bf16)
        near_send[1, n, :, half:width] = (other[:, half:width] + far_in[1, n].astype(f32)).astype(bf16)
        for copy in near_copies(n):
            copy.start()

    def finish(n):
        for copy in near_copies(n):
            copy.wait_recv()
        whole_sum = held[kept(n, chip), :] + near_in[0, n].astype(f32) + near_in[1, n].astype(f32)
        text_out[:, n * width : (n + 1) * width] = whole_sum.astype(bf16)

    for copy in weight_copies:
        copy.wait()
    for t in range(PARTS + 10):
        for lag, stage in ((0, multiply), (3, send_far), (6, send_near), (10, finish)):
            if 0 <= t - lag < PARTS:
                stage(t - lag)
        if 5 <= t < chunks + 5:
            output(t - 5)
    for copy in out_copies:
        copy.wait()
    for n in range(PARTS):
        for copy in (pair_copy(n), *far_copies(n), *near_copies(n)):
            copy.wait_send()

    @pl.when(has_left)
    def _():
        q_copy.wait_send()
        g_copy.wait_send()
        total_copy.wait_send()

    @pl.when(has_next)
    def _():
        stats_copy.wait_send()
        dq_copy.wait_send()


def hand_over_kernel(
    text_in, key_in, value_in, text_out, key_out, value_out, text, keys, values, in_sem, out_sem
):
    held = (text, keys, values)
    arrive = [
        pltpu.make_async_copy(src, dst, in_sem.at[n])
        for n, (src, dst) in enumerate(zip((text_in, key_in, value_in), held))
    ]
    leave = [
        pltpu.make_async_copy(src, dst, out_sem.at[n])
        for n, (src, dst) in enumerate(zip(held, (text_out, key_out, value_out)))
    ]
    for copy in arrive:
        copy.start()
    for first, second in zip(arrive, leave):
        first.wait()
        second.start()
    for copy in leave:
        copy.wait()


def on_device(
    q_raw,
    out_grad,
    q_gain,
    image_keys,
    image_values,
    block_images,
    image_slot,
    tile_counts,
    q_weight,
):
    rows, cols = q_raw.shape
    key_count = image_keys.shape[1]
    padded = -(-key_count // CHUNK) * CHUNK
    chunks = padded // CHUNK
    smem = pl.BlockSpec(memory_space=pltpu.SMEM)
    vmem = pl.BlockSpec(memory_space=pltpu.VMEM)
    hbm = pl.BlockSpec(memory_space=pl.ANY)
    V = pltpu.VMEM
    width = q_weight.shape[0] // PARTS
    weight_rest = q_weight.shape[0] - padded // width * width
    chips = lax.axis_size("tp") // 2
    results = pl.pallas_call(
        attention_kernel,
        out_shape=(
            jax.ShapeDtypeStruct((rows // (2 * chips), q_weight.shape[0]), bf16),
            jax.ShapeDtypeStruct(image_keys.shape, bf16),
            jax.ShapeDtypeStruct(image_values.shape, bf16),
        ),
        in_specs=[smem] * 2 + [vmem] * 3 + [hbm] * 3,
        out_specs=(vmem, hbm, hbm),
        scratch_shapes=[
            V((key_count, HD), bf16),
            V((key_count, HD), bf16),
            V((padded, HD), bf16),
            V((padded, HD), bf16),
            V((HD, padded), bf16),
            V((HD + 16, padded), bf16),
            V((2, HD, cols), bf16),
            V((2, HD, cols), bf16),
            V((2, padded, cols), bf16),
            V((2, chunks, 1, cols), f32),
            V((CHUNK, cols), f32),
            V((cols, CHUNK), bf16),
            V((cols, CHUNK), bf16),
            V((2, HD + 16, cols), f32),
            V((HD, padded), f32),
            V((HD, padded), f32),
            V((2, HD, cols), f32),
            V((8, cols), f32),
            V((8, cols), f32),
            V((8, cols), f32),
            V((1, 8, cols), f32),
            V((8, cols), f32),
            V((HD, cols), bf16),
            V((HD, cols), bf16),
            V((rows, cols), bf16),
            V((weight_rest, cols), bf16),
            V((PARTS, chips, 16, width), bf16),
            V((PARTS, chips, 16, width), bf16),
            V((2, PARTS, 16, width // 2), bf16),
            V((2, PARTS, 16, width // 2), bf16),
            V((2, PARTS, 16, width), bf16),
            V((2, PARTS, 16, width), bf16),
            pltpu.SemaphoreType.DMA((6,)),
            pltpu.SemaphoreType.DMA((5,)),
            pltpu.SemaphoreType.DMA((5,)),
            pltpu.SemaphoreType.DMA((5, PARTS)),
            pltpu.SemaphoreType.DMA((5, PARTS)),
        ],
        compiler_params=pltpu.CompilerParams(
            collective_id=0, has_side_effects=True, vmem_limit_bytes=255 << 18
        ),
        name="attention",
    )(image_slot, tile_counts, q_raw, out_grad, q_gain.reshape(1, HD), image_keys, image_values, q_weight)
    return pl.pallas_call(
        hand_over_kernel,
        out_shape=tuple(jax.ShapeDtypeStruct(x.shape, x.dtype) for x in results),
        in_specs=[hbm] * 3,
        out_specs=(hbm, hbm, hbm),
        scratch_shapes=[V(x.shape, x.dtype) for x in results]
        + [pltpu.SemaphoreType.DMA((3,))] * 2,
        compiler_params=pltpu.CompilerParams(vmem_limit_bytes=63 << 20),
        name="hand_over",
    )(*results)


def solution(mesh):
    return jax.shard_map(
        on_device,
        mesh=mesh,
        in_specs=(
            P("seq", "tp"),
            P("seq", "tp"),
            P(),
            P("seq", None, "tp"),
            P("seq", None, "tp"),
            P(),
            P(),
            P(),
            P(None, "tp"),
        ),
        out_specs=(P(("seq", "tp"), None), P("seq", None, "tp"), P("seq", None, "tp")),
        check_vma=False,
    )
```
